32 devices in a mesh: section: 4 (over z), expert: 8 (over y, x, core).
Axes of the slice: x: 2, y: 2, z: 4, core: 2. Of those that a mesh axis runs over, the one named last changes fastest.
Arguments:
- fwd_sent: bfloat16 [4, 512, 4096], P('section', 'expert'), may hold values from -6 to 6
- bwd_sent: bfloat16 [4, 512, 4096], P('section', 'expert'), may hold values from -6 to 6
- bwd_saved: bfloat16 [4, 512, 4096], P('section', 'expert'), may hold values from -6 to 6
- fwd_routes: int32 [4, 512, 8], P('section', 'expert'), may hold values from 0 to 127, all different within a row; in each aligned block of 64 rows (0 to 63, 64 to 127, ..., all dimensions but the last counted through in order) at most 8 rows name the same one
- bwd_routes: int32 [4, 512, 8], P('section', 'expert'), may hold values from 0 to 127, all different within a row; in each aligned block of 64 rows (0 to 63, 64 to 127, ..., all dimensions but the last counted through in order) at most 8 rows name the same one
- fwd_logits: float32 [4, 512, 128], P('section', 'expert'), may hold values from -3 to 330
- bwd_logits: float32 [4, 512, 128], P('section', 'expert'), may hold values from -3 to 330
- norm_gain: bfloat16 [4, 4096], P('section'), may hold values from 0.5 to 1.5
- w_gate: bfloat16 [4, 4096, 3072], P('section', None, 'expert'), may hold values from -0.09375 to 0.09375
- w_up: bfloat16 [4, 4096, 3072], P('section', None, 'expert'), may hold values from -0.09375 to 0.09375
- w_down: bfloat16 [4, 3072, 4096], P('section', 'expert'), may hold values from -0.4375 to 0.4375
Outputs:
- fwd_out: bfloat16 [4, 512, 4096], P('section', 'expert')
- bwd_out: bfloat16 [4, 512, 4096], P('section', 'expert')
- balance: float32 [4, 128], P('section')
The draws below stay inside these ranges and needn't reach their ends.
Inputs may be any that keep to these rules, and one draw needn't show every extreme that they name: `fwd_routes`: each token names 8 different experts; among the 64 tokens of one index of expert no expert is named more than 8 times, a bound that some block reaches. `bwd_routes`: as for fwd_routes.
All inputs are finite; a program needn't handle non-finite values.
Results may differ from the reference program's by a relative error of at most 0.0045.
Values may be sent and summed in bfloat16 or wider, within the bound.
A program may use at most 64 MiB of HBM per device.

```python
import math
import jax
import jax.numpy as jnp
import numpy as np
from jax import lax

D = 4096
FF_WIN = 1536
EXPERTS = 128
TOPK = 8
EXP_WIN = 2
TOK_DEV = 64
CAP = 8
SECTIONS = 4
TOKENS = 512
H_DEV = 384
N_EXPERT = 8


def draw_logits(key):
    base_key, lead_key = jax.random.split(key, 2)
    shape = (SECTIONS, TOKENS, EXPERTS)
    expert_ids = jnp.arange(EXPERTS, dtype=jnp.int32)
    computed = (expert_ids < EXP_WIN)[None, None, :]
    leading = jax.random.uniform(lead_key, shape, jnp.float32, 1.5, 3.5)
    base = jnp.clip(0.7 * jax.random.normal(base_key, shape, jnp.float32), -2.5, 2.5)
    return jnp.where(computed, leading, base)


def draw_fwd_logits(key, part):
    return draw_logits(jax.random.fold_in(key, 11))


def draw_bwd_logits(key, part):
    return draw_logits(jax.random.fold_in(key, 23))


def steps_of(key, extent, shards, least, largest):
    def one(dim, shards_of):
        heights = jax.random.uniform(jax.random.fold_in(jax.random.fold_in(key, 6), dim), (shards_of,), jnp.float32, least / len(shards), largest / len(shards))
        return jnp.repeat(jnp.exp(heights), extent[dim] // shards_of).reshape((-1,) + (1,) * (len(extent) - dim - 1))

    factor_of = one(*shards[0])
    for cut in shards[1:]:
        factor_of = factor_of * one(*cut)
    return factor_of


def routed_block(rng, own, number, rows, number_of, top, bound, lean):
    ranking = jax.random.permutation(rng, number_of)
    crowded, common = shares(number_of, rows * top, bound, lean, True), shares(number_of, rows * top, bound, lean, False)
    places = jnp.arange(number_of)

    def named(tallies, turn):
        used = int((tallies > 0).sum())
        fixed = max(1, used // 4)
        moved = fixed + (places - fixed + turn * (used - fixed)) % max(1, number_of - fixed)
        return jnp.zeros((number_of,), jnp.int32).at[ranking[jnp.where(places < fixed, places, moved)]].set(jnp.asarray(tallies, jnp.int32))

    tallies = jnp.where(number % 4 == 0, named(crowded, number // 4), named(common, number - number // 4 - 1))
    mixed = jax.random.permutation(jax.random.fold_in(own, 3), number_of)
    giver, taker = mixed[0:number_of // 2 * 2:2], mixed[1:number_of // 2 * 2:2]
    slack = jnp.minimum(tallies[giver] - 1, bound - tallies[taker]) // 2
    slack = jnp.where((giver == ranking[0]) | (taker == ranking[0]) | (tallies[taker] == 0), 0, jnp.maximum(slack, 0))
    moved = jax.random.randint(jax.random.fold_in(own, 4), (number_of // 2,), 0, 1 << 20) % (slack + 1)
    tallies = tallies.at[giver].add(-moved).at[taker].add(moved)
    items = jnp.searchsorted(jnp.cumsum(tallies), jnp.arange(rows * top), side="right").astype(jnp.int32)
    grid = items.reshape(top, rows).T
    grid = grid[jax.random.permutation(jax.random.fold_in(own, 1), rows)]
    turn = jax.random.randint(jax.random.fold_in(own, 2), (rows, 1), 0, top)
    return jnp.take_along_axis(grid, (jnp.arange(top)[None, :] + turn) % top, axis=1)


def shares(number_of, total, most, skew, full):
    weights = [(1 << 20) // math.isqrt(standing ** skew) + 1 for standing in range(1, number_of + 1)]
    largest = most if full else min(most, max(-(-total // number_of), total * weights[0] // sum(weights)))
    least = 1 if total - largest >= number_of - 1 else 0
    holding, surplus = [largest] + [least] * (number_of - 1), total - largest - least * (number_of - 1)
    while surplus > 0:
        movable = [i for i in range(1, number_of) if holding[i] < largest] or [i for i in range(1, number_of) if holding[i] < most]
        pool, left = sum([weights[i] for i in movable]), surplus
        for i in movable:
            more = min(most - holding[i], max(1, left * weights[i] // pool), surplus)
            holding[i] = holding[i] + more
            surplus = surplus - more
    return np.array(holding)


def centred(own_key, shape, deviation, most, pieces=(), held_as=jnp.bfloat16):
    gain = steps_of(own_key, shape, pieces, -0.22, 0.18) if pieces else 1.0
    result = jax.random.normal(own_key, shape, jnp.float32) * deviation * gain
    return jnp.minimum(jnp.maximum(result, -most), most).astype(held_as)


def setup_inputs(seed: int = 0) -> dict:
    key_list = jax.random.split(jax.random.key(seed), 12)
    fwd_sent = centred(key_list[0], (SECTIONS, TOKENS, D), 1.0, 6.0, ((0, 4), (1, 8)))
    bwd_sent = centred(key_list[1], (SECTIONS, TOKENS, D), 1.0, 6.0, ((0, 4), (1, 8)))
    bwd_saved = centred(key_list[2], (SECTIONS, TOKENS, D), 1.0, 6.0, ((0, 4), (1, 8)))
    fwd_routes_keys = jax.random.split(jax.random.fold_in(key_list[3], 1), SECTIONS * TOKENS // TOK_DEV)
    fwd_routes_turns = jax.random.permutation(jax.random.fold_in(key_list[3], 3), SECTIONS * TOKENS // TOK_DEV)
    fwd_routes = jax.vmap(lambda own, number: routed_block(jax.random.fold_in(key_list[3], 2), own, number, TOK_DEV, EXPERTS, TOPK, CAP, 1))(fwd_routes_keys, fwd_routes_turns).reshape((SECTIONS, TOKENS, TOPK))
    bwd_routes_keys = jax.random.split(jax.random.fold_in(key_list[4], 1), SECTIONS * TOKENS // TOK_DEV)
    bwd_routes_turns = jax.random.permutation(jax.random.fold_in(key_list[4], 3), SECTIONS * TOKENS // TOK_DEV)
    bwd_routes = jax.vmap(lambda own, number: routed_block(jax.random.fold_in(key_list[4], 2), own, number, TOK_DEV, EXPERTS, TOPK, CAP, 1))(bwd_routes_keys, bwd_routes_turns).reshape((SECTIONS, TOKENS, TOPK))
    fwd_logits = draw_fwd_logits(jax.random.fold_in(key_list[11], 71), 0)
    bwd_logits = draw_bwd_logits(jax.random.fold_in(key_list[11], 71), 0)
    norm_gain = jnp.clip(0.5 + 1.0 * jax.random.uniform(key_list[7], (SECTIONS, D), jnp.float32) ** steps_of(key_list[7], (SECTIONS, D), ((0, 4),), -0.2, 0.2), 0.5, 1.5).astype(jnp.bfloat16)
    w_gate = centred(key_list[8], (SECTIONS, D, EXP_WIN * FF_WIN), D ** -0.5, 0.09375, ((0, 4), (2, 8)))
    w_up = centred(key_list[9], (SECTIONS, D, EXP_WIN * FF_WIN), D ** -0.5, 0.09375, ((0, 4), (2, 8)))
    w_down = centred(key_list[10], (SECTIONS, EXP_WIN * FF_WIN, D), (FF_WIN // 8) ** -0.5, 0.4375, ((0, 4), (1, 8)))
    return dict(fwd_sent=fwd_sent, bwd_sent=bwd_sent, bwd_saved=bwd_saved, fwd_routes=fwd_routes, bwd_routes=bwd_routes, fwd_logits=fwd_logits, bwd_logits=bwd_logits, norm_gain=norm_gain, w_gate=w_gate, w_up=w_up, w_down=w_down)


epsilon = 1e-06

def norm_rows(values, gain_row):
    widened = values.astype(jnp.float32)
    inverse = lax.rsqrt(lax.optimization_barrier(jnp.mean(widened * widened, axis=-1, keepdims=True)) + epsilon)
    normed = (widened * inverse * gain_row.astype(jnp.float32)).astype(jnp.bfloat16)
    return (normed, widened, inverse)

def slot_tables(routes, logits):
    tokens_here = routes.shape[0]
    chosen = jnp.take_along_axis(logits, routes, axis=1)
    gates = jax.nn.softmax(chosen, axis=1)
    match = (routes[:, :, None] == jnp.arange(EXP_WIN, dtype=jnp.int32)[None, None, :]).astype(jnp.int32)
    flat = match.reshape(tokens_here * TOPK, EXP_WIN)
    earlier = (jnp.cumsum(flat, axis=0) - flat).reshape(tokens_here, TOPK, EXP_WIN)
    placed = match[..., None] * (earlier[..., None] == jnp.arange(CAP, dtype=jnp.int32)).astype(jnp.int32)
    select = lax.optimization_barrier(jnp.sum(placed, axis=1)).astype(jnp.float32)
    gate_slot = lax.optimization_barrier(jnp.sum(placed.astype(jnp.float32) * gates[:, :, None, None], axis=(0, 1)))
    return (select, gate_slot)

def expert_forward(rows, gate_w, up_w, down_w):
    groups = FF_WIN // H_DEV
    gate_pre = jnp.dot(rows, gate_w, preferred_element_type=jnp.float32)
    up_pre = jnp.dot(rows, up_w, preferred_element_type=jnp.float32)
    hidden = (jax.nn.silu(gate_pre) * up_pre).astype(jnp.bfloat16)
    parts = jnp.einsum('rsh,shd->rsd', hidden.reshape(-1, groups, H_DEV).astype(jnp.float32), down_w.reshape(groups, H_DEV, D).astype(jnp.float32))
    parts = lax.optimization_barrier(parts.astype(jnp.bfloat16)).astype(jnp.float32)
    return lax.optimization_barrier(jnp.sum(parts, axis=1))

def expert_backward(rows, grads, gate_w, up_w, down_w):
    groups = FF_WIN // H_DEV
    gate_pre = jnp.dot(rows, gate_w, preferred_element_type=jnp.float32)
    up_pre = jnp.dot(rows, up_w, preferred_element_type=jnp.float32)
    sigma = jax.nn.sigmoid(gate_pre)
    d_hidden = jnp.dot(grads, down_w.T, preferred_element_type=jnp.float32)
    d_gate = (d_hidden * up_pre * sigma * (1.0 + gate_pre * (1.0 - sigma))).astype(jnp.bfloat16)
    d_up = (d_hidden * gate_pre * sigma).astype(jnp.bfloat16)
    parts = jnp.einsum('rsh,dsh->rsd', d_gate.reshape(-1, groups, H_DEV).astype(jnp.float32), gate_w.reshape(D, groups, H_DEV).astype(jnp.float32))
    parts = parts + jnp.einsum('rsh,dsh->rsd', d_up.reshape(-1, groups, H_DEV).astype(jnp.float32), up_w.reshape(D, groups, H_DEV).astype(jnp.float32))
    parts = lax.optimization_barrier(parts.astype(jnp.bfloat16)).astype(jnp.float32)
    return lax.optimization_barrier(jnp.sum(parts, axis=1))

def one_section(packed):
    x_in, upstream, saved, froutes, broutes, flogits, blogits, gain_row, gate_w, up_w, down_w = packed
    blocks = N_EXPERT
    normed = norm_rows(x_in, gain_row)[0]
    fsel, fgate = jax.vmap(slot_tables)(froutes.reshape(blocks, TOK_DEV, TOPK), flogits.reshape(blocks, TOK_DEV, EXPERTS))
    frows = jnp.einsum('btec,btd->becd', fsel, normed.reshape(blocks, TOK_DEV, D).astype(jnp.float32)).astype(jnp.bfloat16)
    fexp = jnp.stack([expert_forward(frows[:, e].reshape(blocks * CAP, D), gate_w[:, e * FF_WIN:(e + 1) * FF_WIN], up_w[:, e * FF_WIN:(e + 1) * FF_WIN], down_w[e * FF_WIN:(e + 1) * FF_WIN, :]).reshape(blocks, CAP, D) for e in range(EXP_WIN)], axis=1)
    mixed = jnp.einsum('btec,becd->btd', fsel * fgate[:, None], fexp).reshape(TOKENS, D)
    fwd_out = (x_in.astype(jnp.float32) + mixed).astype(jnp.bfloat16)
    saved_normed, saved_wide, saved_inv = norm_rows(saved, gain_row)
    bsel, bgate = jax.vmap(slot_tables)(broutes.reshape(blocks, TOK_DEV, TOPK), blogits.reshape(blocks, TOK_DEV, EXPERTS))
    brows = jnp.einsum('btec,btd->becd', bsel, saved_normed.reshape(blocks, TOK_DEV, D).astype(jnp.float32)).astype(jnp.bfloat16)
    grows = jnp.einsum('btec,btd->becd', bsel, upstream.reshape(blocks, TOK_DEV, D).astype(jnp.float32))
    grows = (grows * bgate[..., None]).astype(jnp.bfloat16)
    bexp = jnp.stack([expert_backward(brows[:, e].reshape(blocks * CAP, D), grows[:, e].reshape(blocks * CAP, D), gate_w[:, e * FF_WIN:(e + 1) * FF_WIN], up_w[:, e * FF_WIN:(e + 1) * FF_WIN], down_w[e * FF_WIN:(e + 1) * FF_WIN, :]).reshape(blocks, CAP, D) for e in range(EXP_WIN)], axis=1)
    d_normed = jnp.einsum('btec,becd->btd', bsel, bexp).reshape(TOKENS, D)
    weighted = gain_row.astype(jnp.float32) * d_normed
    d_saved = saved_inv * weighted - saved_wide * saved_inv ** 3 * lax.optimization_barrier(jnp.mean(saved_wide * weighted, axis=-1, keepdims=True))
    bwd_out = (upstream.astype(jnp.float32) + d_saved).astype(jnp.bfloat16)
    counts = lax.optimization_barrier(jnp.sum((froutes[:, :, None] == jnp.arange(EXPERTS, dtype=jnp.int32)[None, None, :]).astype(jnp.float32), axis=(0, 1)))
    prob_sums = lax.optimization_barrier(jnp.sum(jax.nn.softmax(flogits, axis=1), axis=0))
    balance = EXPERTS * (counts / (TOKENS * TOPK)) * (prob_sums / TOKENS)
    return (fwd_out, bwd_out, balance)

def reference(fwd_sent, bwd_sent, bwd_saved, fwd_routes, bwd_routes, fwd_logits, bwd_logits, norm_gain, w_gate, w_up, w_down):
    x_all = jnp.roll(fwd_sent, 1, axis=0)
    upstream_all = jnp.roll(bwd_sent, -1, axis=0)
    fwd_out, bwd_out, balance = lax.map(one_section, (x_all, upstream_all, bwd_saved, fwd_routes, bwd_routes, fwd_logits, bwd_logits, norm_gain, w_gate, w_up, w_down))
    return (fwd_out, bwd_out, balance)
```

```python
import functools

import jax
import jax.numpy as jnp
from jax import lax
from jax.experimental import pallas as pl
from jax.experimental.pallas import tpu as pltpu
from jax.sharding import PartitionSpec as P

EXPERTS = 128
TOPK = 8
EXP_WIN = 2
CAP = 8
SLOTS = EXP_WIN * CAP
HEAD = 16
CHUNK = 512
EPSILON = 1e-06
MESH = pl.DeviceIdType.MESH
F32 = jnp.float32
BF16 = jnp.bfloat16
NT = (((1,), (1,)), ((), ()))


def iota(shape, dim):
    return lax.broadcasted_iota(jnp.int32, shape, dim)


def dot(a, b):
    return jnp.dot(a, b, preferred_element_type=F32)


def columns(width, body, init=0):
    def step(i, carry):
        return body(pl.ds(pl.multiple_of(i * CHUNK, CHUNK), CHUNK), carry)

    return lax.fori_loop(0, width // CHUNK, step, init)


def route_tables(routes, logits):
    tokens, experts = logits.shape
    lane = iota((tokens, experts), 1)
    chosen = routes[:, 0:1] == lane
    for k in range(1, TOPK):
        chosen = chosen | (routes[:, k : k + 1] == lane)
    hit = chosen.astype(F32)
    top = jnp.max(jnp.where(chosen, logits, -jnp.inf), axis=1, keepdims=True)
    raised = jnp.exp(jnp.where(chosen, logits, top) - top) * hit
    gates = raised / jnp.sum(raised, axis=1, keepdims=True)
    here = jnp.max(jnp.where(lane < EXP_WIN, hit, 0.0), axis=1, keepdims=True)
    marks = jnp.where(lane < EXP_WIN, hit, jnp.where(lane == EXP_WIN, here, 0.0))
    below = (iota((tokens, tokens), 1) < iota((tokens, tokens), 0)).astype(BF16)
    earlier = dot(below, marks.astype(BF16))
    before = earlier[:, EXP_WIN : EXP_WIN + 1]
    count = jnp.sum(here, axis=0, keepdims=True)
    place = jnp.where(
        here > 0.0, before, count + iota((tokens, 1), 0).astype(F32) - before
    )

    def slot_at(slot):
        taken = jnp.zeros(slot.shape, F32)
        gated = jnp.zeros(slot.shape, F32)
        for e in range(EXP_WIN):
            there = (slot // CAP == e) & (
                earlier[:, e : e + 1] == (slot - e * CAP).astype(F32)
            )
            mine = jnp.where(there, hit[:, e : e + 1], 0.0)
            taken = taken + mine
            gated = gated + mine * gates[:, e : e + 1]
        return taken, gated

    taken, gated = slot_at(lane)
    taken = jnp.where(lane < SLOTS, taken, 0.0)
    gated = jnp.where(lane < SLOTS, gated, 0.0)
    taken = jnp.where(lane == SLOTS, place, taken)
    turned = jnp.concatenate([taken, gated], axis=0).T
    select = turned[:SLOTS, :tokens].astype(BF16)
    right = iota((SLOTS, 2 * tokens), 1) >= tokens
    gate_slot = jnp.sum(jnp.where(right, turned[:SLOTS], 0.0), axis=1, keepdims=True)
    place_row = turned[SLOTS : SLOTS + 1]
    again = lane - tokens
    again = jnp.where(again >= SLOTS, again - SLOTS, again)
    back = jnp.where(
        lane < tokens,
        (place == lane.astype(F32)).astype(F32),
        jnp.where(lane < tokens + 2 * SLOTS, slot_at(again)[0], 0.0),
    ).astype(BF16)
    head_select = dot(select, back[:, :HEAD]).astype(BF16)
    return hit, select, head_select, gate_slot, place_row, back[:, : tokens + 2 * SLOTS]


def permutation(place_row, tokens):
    return (iota((tokens, tokens), 0).astype(F32) == place_row[:, :tokens]).astype(BF16)


def halves(rows):
    high = rows.astype(BF16)
    return high, (rows - high.astype(F32)).astype(BF16)


def kernel(
    sections, n,
    fwd_ref, bwd_ref, saved_ref, froute_ref, broute_ref, flogit_ref, blogit_ref, gain_ref,
    wg_hbm, wu_hbm, wd_hbm,
    fout_ref, bout_ref, balance_ref,
    wg, wu, wd, place_out, place_in, head_out, tail_out, head_in, tail_in,
    slab, rx, part, pair_in, summed, home, raw, wide, terms, stats,
    w_sem, z_send, z_recv, d_send, d_recv, f_send, f_recv,
    p_send, p_recv, h_send, h_recv, s_send, s_recv,
):
    tokens, width = fwd_ref.shape
    half = n // 2
    span = half // EXP_WIN
    sec, me = lax.axis_index("section"), lax.axis_index("expert")
    core, mine = lax.rem(me, 2), me // 2
    sibling = me + 1 - 2 * core
    after, ahead = lax.rem(sec + 1, sections), lax.rem(sec + sections - 1, sections)

    loads = [
        pltpu.make_async_copy(src, dst, w_sem.at[i])
        for i, (src, dst) in enumerate(((wg_hbm, wg), (wu_hbm, wu), (wd_hbm, wd)))
    ]
    for load in loads:
        load.start()

    barrier = pltpu.get_barrier_semaphore()
    for d in range(1, n):
        pl.semaphore_signal(
            barrier, inc=1, device_id={"expert": lax.rem(me + d, n)}, device_id_type=MESH
        )
    for where in (after, ahead):
        pl.semaphore_signal(barrier, inc=1, device_id={"section": where}, device_id_type=MESH)

    hit, _, f_pick, f_gate, f_place, f_back = route_tables(froute_ref[...], flogit_ref[...])
    _, b_select, b_pick, b_gate, b_place, b_back = route_tables(broute_ref[...], blogit_ref[...])
    place_out[0] = jnp.broadcast_to(f_place, place_out.shape[1:])
    place_out[1] = jnp.broadcast_to(b_place, place_out.shape[1:])
    logits = flogit_ref[...]
    raised = jnp.exp(logits - jnp.max(logits, axis=1, keepdims=True))
    probs = raised / jnp.sum(raised, axis=1, keepdims=True)
    both = jnp.concatenate(
        [jnp.sum(hit, axis=0, keepdims=True), jnp.sum(probs, axis=0, keepdims=True)], axis=0
    )
    row = iota((8, EXPERTS), 0)
    stats[me] = jnp.where(row == 0, both[0:1], jnp.where(row == 1, both[1:2], 0.0))

    pl.semaphore_wait(barrier, n + 1)

    def z_copy(which, src, dst, where):
        return pltpu.make_async_remote_copy(
            src_ref=src, dst_ref=dst, send_sem=z_send.at[which], recv_sem=z_recv.at[which],
            device_id={"section": where}, device_id_type=MESH,
        )

    places = [
        z_copy(0, place_out.at[0], place_in.at[0], ahead),
        z_copy(1, place_out.at[1], place_in.at[1], after),
    ]
    heads = [
        z_copy(2, head_out.at[0], head_in.at[0], after),
        z_copy(3, head_out.at[1], head_in.at[1], ahead),
    ]
    tails = [
        z_copy(4, tail_out.at[0], tail_in.at[0], after),
        z_copy(5, tail_out.at[1], tail_in.at[1], ahead),
    ]
    for copy in places:
        copy.start()

    def peer(d):
        return lax.rem(mine + d, half)

    def direct(kind, d):
        other = peer(d)
        return pltpu.make_async_remote_copy(
            src_ref=slab.at[kind, other // span], dst_ref=rx.at[kind, core, mine],
            send_sem=d_send.at[kind, other], recv_sem=d_recv.at[kind, mine],
            device_id={"expert": 2 * other + core}, device_id_type=MESH,
        )

    def arrival(kind, d):
        other = peer(d)
        return pltpu.make_async_remote_copy(
            src_ref=slab.at[kind, 0], dst_ref=rx.at[kind, core, other],
            send_sem=d_send.at[kind, other], recv_sem=d_recv.at[kind, other],
            device_id={"expert": 2 * other + core}, device_id_type=MESH,
        )

    def forward(kind, side, other):
        return pltpu.make_async_remote_copy(
            src_ref=rx.at[kind, side, other], dst_ref=rx.at[kind, side, other],
            send_sem=f_send.at[kind, other], recv_sem=f_recv.at[kind, other],
            device_id={"expert": sibling}, device_id_type=MESH,
        )

    def dispatch(kind):
        for d in range(1, half):
            direct(kind, d).start()
        rx[kind, core, mine] = slab[kind, mine // span]
        forward(kind, core, mine).start()

    def relay(kind):
        for d in range(1, half):
            arrival(kind, d).wait_recv()
            forward(kind, core, peer(d)).start()

    def complete(kind):
        for d in range(half):
            forward(kind, 1 - core, peer(d)).wait_recv()

    def to_slab(kind, rows, at):
        for e in range(EXP_WIN):
            slab[kind, e, :, at] = rows[e * CAP : (e + 1) * CAP].astype(BF16)

    def gather_saved(at, total):
        rows = dot(b_select, saved_ref[:, at])
        raw[:, at] = rows
        return total + jnp.sum(rows * rows, axis=1, keepdims=True)

    square = columns(width, gather_saved, jnp.zeros((SLOTS, 1), F32))
    saved_inv = lax.rsqrt(square / width + EPSILON)

    def norm_saved(at, carry):
        to_slab(0, raw[:, at] * saved_inv * gain_ref[:, at].astype(F32), at)
        return carry

    columns(width, norm_saved)
    dispatch(0)

    sources = (fwd_ref, bwd_ref)
    orders = []
    for which in range(2):
        places[which].wait_recv()
        orders.append(permutation(place_in[which, 0:1], tokens))

    for which in range(2):
        def fill_head(at, carry, which=which):
            head_out[which, :, at] = dot(orders[which][:HEAD], sources[which][:, at]).astype(BF16)
            return carry

        columns(width, fill_head)
        heads[which].start()
    for which in range(2):
        def fill_tail(at, carry, which=which):
            tail_out[which, :, at] = dot(orders[which][HEAD:], sources[which][:, at]).astype(BF16)
            return carry

        columns(width, fill_tail)
        tails[which].start()

    def stat(d):
        other = lax.rem(me + d, n)
        return pltpu.make_async_remote_copy(
            src_ref=stats.at[me], dst_ref=stats.at[me],
            send_sem=s_send.at[other], recv_sem=s_recv.at[me],
            device_id={"expert": other}, device_id_type=MESH,
        )

    def stat_arrival(d):
        other = lax.rem(me + d, n)
        return pltpu.make_async_remote_copy(
            src_ref=stats.at[other], dst_ref=stats.at[other],
            send_sem=s_send.at[other], recv_sem=s_recv.at[other],
            device_id={"expert": other}, device_id_type=MESH,
        )

    for d in range(1, n):
        stat(d).start()

    def arrived(kind, at):
        return rx[kind, :, :, :, at].astype(F32).reshape(n * CAP, CHUNK).astype(BF16)

    hidden = wg.shape[1]
    zero = jnp.zeros((n * CAP, hidden), F32)

    def gate_up(kind):
        def step(at, carry):
            rows = arrived(kind, at)
            return carry[0] + dot(rows, wg[at, :]), carry[1] + dot(rows, wu[at, :])

        return columns(width, step, (zero, zero))

    relay(0)
    loads[0].wait()
    loads[1].wait()
    complete(0)
    gate_b, up_b = gate_up(0)
    sigma = jax.nn.sigmoid(gate_b)
    terms[0] = up_b * sigma * (1.0 + gate_b * (1.0 - sigma))
    terms[1] = gate_b * sigma

    heads[1].wait_recv()

    def gather_grads(at, carry):
        to_slab(1, dot(b_pick, head_in[1, :, at]) * b_gate, at)
        return carry

    columns(width, gather_grads)
    dispatch(1)

    heads[0].wait_recv()

    def gather_fwd(at, total):
        rows = dot(f_pick, head_in[0, :, at])
        wide[:, at] = rows
        return total + jnp.sum(rows * rows, axis=1, keepdims=True)

    square = columns(width, gather_fwd, jnp.zeros((SLOTS, 1), F32))
    fwd_inv = lax.rsqrt(square / width + EPSILON)

    def norm_fwd(at, carry):
        to_slab(2, wide[:, at] * fwd_inv * gain_ref[:, at].astype(F32), at)
        return carry

    columns(width, norm_fwd)
    dispatch(2)
    relay(1)
    relay(2)
    loads[2].wait()
    complete(1)

    def pair(which):
        return pltpu.make_async_remote_copy(
            src_ref=part.at[which, 1 - core], dst_ref=pair_in.at[which],
            send_sem=p_send.at[which], recv_sem=p_recv.at[which],
            device_id={"expert": sibling}, device_id_type=MESH,
        )

    def to_home(which, d):
        other = peer(d)
        return pltpu.make_async_remote_copy(
            src_ref=summed.at[which, other], dst_ref=home.at[which, mine],
            send_sem=h_send.at[which, other], recv_sem=h_recv.at[which, mine],
            device_id={"expert": 2 * other + core}, device_id_type=MESH,
        )

    def from_holder(which, d):
        other = peer(d)
        return pltpu.make_async_remote_copy(
            src_ref=summed.at[which, other], dst_ref=home.at[which, other],
            send_sem=h_send.at[which, other], recv_sem=h_recv.at[which, other],
            device_id={"expert": 2 * other + core}, device_id_type=MESH,
        )

    def keep(which, rows, at):
        part[which, :, :, :, at] = rows.reshape(2, half, CAP, CHUNK).astype(BF16)

    def give(which):
        pair(which).wait_recv()

        def add(at, carry):
            total = part[which, core, :, :, at].astype(F32) + pair_in[which, :, :, at].astype(F32)
            summed[which, :, :, at] = total.astype(BF16)
            return carry

        columns(width, add)
        for d in range(1, half):
            to_home(which, d).start()
        home[which, mine] = summed[which, mine]

    d_hidden = columns(
        width,
        lambda at, total: total
        + lax.dot_general(arrived(1, at), wd[:, at], NT, preferred_element_type=F32),
        zero,
    )
    d_gate = (d_hidden * terms[0]).astype(BF16)
    d_up = (d_hidden * terms[1]).astype(BF16)

    def input_grad(at, carry):
        rows = lax.dot_general(d_gate, wg[at, :], NT, preferred_element_type=F32)
        rows = rows + lax.dot_general(d_up, wu[at, :], NT, preferred_element_type=F32)
        keep(0, rows, at)
        return carry

    columns(width, input_grad)
    pair(0).start()

    complete(2)
    gate_f, up_f = gate_up(2)
    hidden_rows = (gate_f * jax.nn.sigmoid(gate_f) * up_f).astype(BF16)
    give(0)

    def down(at, carry):
        keep(1, dot(hidden_rows, wd[:, at]), at)
        return carry

    columns(width, down)
    pair(1).start()

    for d in range(1, n):
        stat_arrival(d).wait_recv()
    counts = stats[0]
    for i in range(1, n):
        counts = counts + stats[i]
    tokens_all = tokens * n
    balance_ref[...] = (
        EXPERTS * (counts[0:1] / (tokens_all * TOPK)) * (counts[1:2] / tokens_all)
    )
    give(1)

    def returned(which, at):
        rows = []
        for e in range(EXP_WIN):
            total = home[which, e * span, :, at].astype(F32)
            for i in range(1, span):
                total = total + home[which, e * span + i, :, at].astype(F32)
            rows.append(total)
        return jnp.concatenate(rows, axis=0)

    def combine(back, which, rows, at):
        high, low = halves(rows)
        stack = jnp.concatenate([head_in[which, :, at], tail_in[which, :, at], high, low], axis=0)
        return dot(back, stack).astype(BF16)

    for d in range(1, half):
        from_holder(0, d).wait_recv()

    def weigh(at, total):
        weighted = returned(0, at) * gain_ref[:, at].astype(F32)
        wide[:, at] = weighted
        return total + jnp.sum(weighted * raw[:, at], axis=1, keepdims=True)

    mean = columns(width, weigh, jnp.zeros((SLOTS, 1), F32)) / width
    scale = saved_inv * saved_inv * saved_inv * mean
    tails[1].wait_recv()

    def finish_bwd(at, carry):
        rows = saved_inv * wide[:, at] - raw[:, at] * scale
        bout_ref[:, at] = combine(b_back, 1, rows, at)
        return carry

    columns(width, finish_bwd)

    for d in range(1, half):
        from_holder(1, d).wait_recv()
    tails[0].wait_recv()

    def finish_fwd(at, carry):
        fout_ref[:, at] = combine(f_back, 0, returned(1, at) * f_gate, at)
        return carry

    columns(width, finish_fwd)

    for copy in places + heads + tails:
        copy.wait_send()
    for kind in range(3):
        for d in range(half):
            forward(kind, core, peer(d)).wait_send()
        for d in range(1, half):
            direct(kind, d).wait_send()
    for which in range(2):
        pair(which).wait_send()
        for d in range(1, half):
            to_home(which, d).wait_send()
    for d in range(1, n):
        stat(d).wait_send()


def body(
    sections, n,
    fwd_sent, bwd_sent, bwd_saved, fwd_routes, bwd_routes, fwd_logits, bwd_logits,
    norm_gain, w_gate, w_up, w_down,
):
    tokens, width = fwd_sent.shape[1:]
    hidden = w_gate.shape[2]
    half = n // 2
    vmem = pl.BlockSpec(memory_space=pltpu.VMEM)
    hbm = pl.BlockSpec(memory_space=pl.ANY)
    dma = pltpu.SemaphoreType.DMA
    fwd_out, bwd_out, balance = pl.pallas_call(
        functools.partial(kernel, sections, n),
        out_shape=(
            jax.ShapeDtypeStruct((tokens, width), BF16),
            jax.ShapeDtypeStruct((tokens, width), BF16),
            jax.ShapeDtypeStruct((1, EXPERTS), F32),
        ),
        in_specs=[vmem] * 8 + [hbm] * 3,
        out_specs=(vmem, vmem, vmem),
        scratch_shapes=[
            pltpu.VMEM((width, hidden), BF16),
            pltpu.VMEM((width, hidden), BF16),
            pltpu.VMEM((hidden, width), BF16),
            pltpu.VMEM((2, 8, 2 * tokens), F32),
            pltpu.VMEM((2, 8, 2 * tokens), F32),
            pltpu.VMEM((2, HEAD, width), BF16),
            pltpu.VMEM((2, tokens - HEAD, width), BF16),
            pltpu.VMEM((2, HEAD, width), BF16),
            pltpu.VMEM((2, tokens - HEAD, width), BF16),
            pltpu.VMEM((3, EXP_WIN, CAP, width), BF16),
            pltpu.VMEM((3, 2, half, CAP, width), BF16),
            pltpu.VMEM((2, 2, half, CAP, width), BF16),
            pltpu.VMEM((2, half, CAP, width), BF16),
            pltpu.VMEM((2, half, CAP, width), BF16),
            pltpu.VMEM((2, half, CAP, width), BF16),
            pltpu.VMEM((SLOTS, width), F32),
            pltpu.VMEM((SLOTS, width), F32),
            pltpu.VMEM((2, n * CAP, hidden), F32),
            pltpu.VMEM((n, 8, EXPERTS), F32),
            dma((3,)), dma((6,)), dma((6,)),
            dma((3, half)), dma((3, half)), dma((3, half)), dma((3, half)),
            dma((2,)), dma((2,)), dma((2, half)), dma((2, half)),
            dma((n,)), dma((n,)),
        ],
        compiler_params=pltpu.CompilerParams(
            collective_id=0, has_side_effects=True, vmem_limit_bytes=52 * 1024 * 1024
        ),
    )(
        fwd_sent[0], bwd_sent[0], bwd_saved[0], fwd_routes[0], bwd_routes[0],
        fwd_logits[0], bwd_logits[0], norm_gain, w_gate[0], w_up[0], w_down[0],
    )
    return fwd_out[None], bwd_out[None], balance


def solution(mesh):
    block = P("section", "expert", None)
    return jax.shard_map(
        functools.partial(body, mesh.shape["section"], mesh.shape["expert"]),
        mesh=mesh,
        in_specs=(block,) * 7
        + (
            P("section", None),
            P("section", None, "expert"),
            P("section", None, "expert"),
            P("section", "expert", None),
        ),
        out_specs=(block, block, P("section", None)),
        check_vma=False,
    )
```

```python
import functools

import jax
import jax.numpy as jnp
from jax import lax
from jax.experimental import pallas as pl
from jax.experimental.pallas import tpu as pltpu
from jax.sharding import PartitionSpec as P

EXPERTS = 128
TOPK = 8
EXP_WIN = 2
CAP = 8
SLOTS = EXP_WIN * CAP
HEAD = 16
CHUNK = 512
PIECES = 2
EPSILON = 1e-06
MESH = pl.DeviceIdType.MESH
F32 = jnp.float32
BF16 = jnp.bfloat16
NT = (((1,), (1,)), ((), ()))


def iota(shape, dim):
    return lax.broadcasted_iota(jnp.int32, shape, dim)


def dot(a, b):
    return jnp.dot(a, b, preferred_element_type=F32)


def columns(width, body, init=0):
    def step(i, carry):
        return body(pl.ds(pl.multiple_of(i * CHUNK, CHUNK), CHUNK), carry)

    return lax.fori_loop(0, width // CHUNK, step, init)


def route_tables(routes, logits):
    tokens, experts = logits.shape
    lane = iota((tokens, experts), 1)
    unit = (iota((tokens, tokens), 0) == iota((tokens, tokens), 1)).astype(BF16)
    routes = lax.dot_general(
        unit, routes.astype(F32).astype(BF16), NT, preferred_element_type=F32
    )
    chosen = routes[:, 0:1] == lane.astype(F32)
    for k in range(1, TOPK):
        chosen = chosen | (routes[:, k : k + 1] == lane.astype(F32))
    hit = chosen.astype(F32)
    top = jnp.max(jnp.where(chosen, logits, -jnp.inf), axis=1, keepdims=True)
    raised = jnp.exp(jnp.where(chosen, logits, top) - top) * hit
    gates = raised / jnp.sum(raised, axis=1, keepdims=True)
    here = jnp.max(jnp.where(lane < EXP_WIN, hit, 0.0), axis=1, keepdims=True)
    marks = jnp.where(lane < EXP_WIN, hit, jnp.where(lane == EXP_WIN, here, 0.0))
    below = (iota((tokens, tokens), 1) < iota((tokens, tokens), 0)).astype(BF16)
    earlier = dot(below, marks.astype(BF16))
    before = earlier[:, EXP_WIN : EXP_WIN + 1]
    count = jnp.sum(here, axis=0, keepdims=True)
    place = jnp.where(
        here > 0.0, before, count + iota((tokens, 1), 0).astype(F32) - before
    )

    def slot_at(slot):
        taken = jnp.zeros(slot.shape, F32)
        gated = jnp.zeros(slot.shape, F32)
        for e in range(EXP_WIN):
            there = (slot // CAP == e) & (
                earlier[:, e : e + 1] == (slot - e * CAP).astype(F32)
            )
            mine = jnp.where(there, hit[:, e : e + 1], 0.0)
            taken = taken + mine
            gated = gated + mine * gates[:, e : e + 1]
        return taken, gated

    taken, gated = slot_at(lane)
    taken = jnp.where(lane < SLOTS, taken, 0.0)
    gated = jnp.where(lane < SLOTS, gated, 0.0)
    turned = jnp.concatenate([taken, gated], axis=0).T
    select = turned[:SLOTS, :tokens].astype(BF16)
    right = iota((SLOTS, 2 * tokens), 1) >= tokens
    gate_slot = jnp.sum(jnp.where(right, turned[:SLOTS], 0.0), axis=1, keepdims=True)
    again = lane - tokens
    again = jnp.where(again >= SLOTS, again - SLOTS, again)
    back = jnp.where(
        lane < tokens,
        (place == lane.astype(F32)).astype(F32),
        jnp.where(lane < tokens + 2 * SLOTS, slot_at(again)[0], 0.0),
    ).astype(BF16)
    head_select = dot(select, back[:, :HEAD]).astype(BF16)
    return hit, select, head_select, gate_slot, back[:, : tokens + 2 * SLOTS]


def place_row(routes):
    tokens = routes.shape[1]
    here = jnp.max(jnp.where(routes < EXP_WIN, 1.0, 0.0), axis=0, keepdims=True)
    here = jnp.broadcast_to(here, (8, tokens))
    above = (iota((tokens, tokens), 0) < iota((tokens, tokens), 1)).astype(BF16)
    before = dot(here.astype(BF16), above)
    count = jnp.sum(here, axis=1, keepdims=True)
    order = iota((8, tokens), 1).astype(F32)
    return jnp.where(here > 0.0, before, count + order - before)


def permutation(place, tokens):
    return (iota((tokens, tokens), 0).astype(F32) == place).astype(BF16)


def halves(rows):
    high = rows.astype(BF16)
    return high, (rows - high.astype(F32)).astype(BF16)


def kernel(
    sections, n,
    froute_hbm, broute_hbm, flogit_hbm, blogit_hbm, fwd_hbm, bwd_hbm, saved_hbm, gain_hbm,
    wg_hbm, wu_hbm, wd_hbm,
    fout_ref, bout_ref, balance_ref,
    froute_ref, broute_ref, flogit_ref, blogit_ref, fwd_ref, bwd_ref, saved_ref, gain_ref,
    wg, wu, wd, place_out, place_in, head_out, tail_out, head_in, tail_in,
    slab, rx, part, pair_in, summed, home, raw, wide, terms, stats,
    w_sem, z_send, z_recv, d_send, d_recv, f_send, f_recv,
    p_send, p_recv, h_send, h_recv, s_send, s_recv,
):
    tokens, width = fwd_ref.shape
    half = n // 2
    span = half // EXP_WIN
    sec, me = lax.axis_index("section"), lax.axis_index("expert")
    core, mine = lax.rem(me, 2), me // 2
    sibling = me + 1 - 2 * core
    after, ahead = lax.rem(sec + 1, sections), lax.rem(sec + sections - 1, sections)

    loads = [
        pltpu.make_async_copy(src, dst, w_sem.at[i])
        for i, (src, dst) in enumerate((
            (froute_hbm, froute_ref), (broute_hbm, broute_ref),
            (flogit_hbm, flogit_ref), (blogit_hbm, blogit_ref),
            (fwd_hbm, fwd_ref), (bwd_hbm, bwd_ref), (saved_hbm, saved_ref), (gain_hbm, gain_ref),
            (wg_hbm, wg), (wu_hbm, wu), (wd_hbm, wd),
        ))
    ]
    for load in loads:
        load.start()

    barrier = pltpu.get_barrier_semaphore()
    for d in range(1, n):
        pl.semaphore_signal(
            barrier, inc=1, device_id={"expert": lax.rem(me + d, n)}, device_id_type=MESH
        )
    for where in (after, ahead):
        pl.semaphore_signal(barrier, inc=1, device_id={"section": where}, device_id_type=MESH)

    loads[0].wait()
    loads[1].wait()
    place_out[0] = place_row(froute_ref[...])
    place_out[1] = place_row(broute_ref[...])
    pl.semaphore_wait(barrier, n + 1)

    def z_copy(which, src, dst, where):
        return pltpu.make_async_remote_copy(
            src_ref=src, dst_ref=dst, send_sem=z_send.at[which], recv_sem=z_recv.at[which],
            device_id={"section": where}, device_id_type=MESH,
        )

    places = [
        z_copy(0, place_out.at[0], place_in.at[0], ahead),
        z_copy(1, place_out.at[1], place_in.at[1], after),
    ]
    heads = [
        z_copy(2, head_out.at[0], head_in.at[0], after),
        z_copy(3, head_out.at[1], head_in.at[1], ahead),
    ]
    tails = [
        z_copy(4, tail_out.at[0], tail_in.at[0], after),
        z_copy(5, tail_out.at[1], tail_in.at[1], ahead),
    ]
    for copy in places:
        copy.start()

    loads[2].wait()
    loads[3].wait()
    hit, _, f_pick, f_gate, f_back = route_tables(froute_ref[...], flogit_ref[...])
    _, b_select, b_pick, b_gate, b_back = route_tables(broute_ref[...], blogit_ref[...])

    def peer(d):
        return lax.rem(mine + d, half)

    def direct(kind, d):
        other = peer(d)
        return pltpu.make_async_remote_copy(
            src_ref=slab.at[kind, other // span], dst_ref=rx.at[kind, core, mine],
            send_sem=d_send.at[kind, other], recv_sem=d_recv.at[kind, mine],
            device_id={"expert": 2 * other + core}, device_id_type=MESH,
        )

    def arrival(kind, d):
        other = peer(d)
        return pltpu.make_async_remote_copy(
            src_ref=slab.at[kind, 0], dst_ref=rx.at[kind, core, other],
            send_sem=d_send.at[kind, other], recv_sem=d_recv.at[kind, other],
            device_id={"expert": 2 * other + core}, device_id_type=MESH,
        )

    def forward(kind, side, other):
        return pltpu.make_async_remote_copy(
            src_ref=rx.at[kind, side, other], dst_ref=rx.at[kind, side, other],
            send_sem=f_send.at[kind, other], recv_sem=f_recv.at[kind, other],
            device_id={"expert": sibling}, device_id_type=MESH,
        )

    def dispatch(kind):
        for d in range(1, half):
            direct(kind, d).start()
        rx[kind, core, mine] = slab[kind, mine // span]
        forward(kind, core, mine).start()

    def relay(kind):
        for d in range(1, half):
            arrival(kind, d).wait_recv()
            forward(kind, core, peer(d)).start()

    def complete(kind):
        for d in range(half):
            forward(kind, 1 - core, peer(d)).wait_recv()

    def to_slab(kind, rows, at):
        for e in range(EXP_WIN):
            slab[kind, e, :, at] = rows[e * CAP : (e + 1) * CAP].astype(BF16)

    loads[4].wait()
    loads[5].wait()
    sources = (fwd_ref, bwd_ref)
    orders = []
    for which in range(2):
        places[which].wait_recv()
        orders.append(permutation(place_in[which, 0:1], tokens))

    for which in range(2):
        def fill_head(at, carry, which=which):
            head_out[which, :, at] = dot(orders[which][:HEAD], sources[which][:, at]).astype(BF16)
            return carry

        columns(width, fill_head)
        heads[which].start()

    loads[6].wait()
    loads[7].wait()

    def gather_saved(at, total):
        rows = dot(b_select, saved_ref[:, at])
        raw[:, at] = rows
        return total + jnp.sum(rows * rows, axis=1, keepdims=True)

    square = columns(width, gather_saved, jnp.zeros((SLOTS, 1), F32))
    saved_inv = lax.rsqrt(square / width + EPSILON)

    def norm_saved(at, carry):
        to_slab(0, raw[:, at] * saved_inv * gain_ref[:, at].astype(F32), at)
        return carry

    columns(width, norm_saved)
    dispatch(0)

    for which in range(2):
        def fill_tail(at, carry, which=which):
            tail_out[which, :, at] = dot(orders[which][HEAD:], sources[which][:, at]).astype(BF16)
            return carry

        columns(width, fill_tail)

    logits = flogit_ref[...]
    raised = jnp.exp(logits - jnp.max(logits, axis=1, keepdims=True))
    probs = raised / jnp.sum(raised, axis=1, keepdims=True)
    count_row = jnp.sum(hit, axis=0, keepdims=True)
    prob_row = jnp.sum(probs, axis=0, keepdims=True)
    row = iota((8, EXPERTS), 0)
    stats[me] = jnp.where(row == 0, count_row, jnp.where(row == 1, prob_row, 0.0))

    def stat(d):
        other = lax.rem(me + d, n)
        return pltpu.make_async_remote_copy(
            src_ref=stats.at[me], dst_ref=stats.at[me],
            send_sem=s_send.at[other], recv_sem=s_recv.at[me],
            device_id={"expert": other}, device_id_type=MESH,
        )

    def stat_arrival(d):
        other = lax.rem(me + d, n)
        return pltpu.make_async_remote_copy(
            src_ref=stats.at[other], dst_ref=stats.at[other],
            send_sem=s_send.at[other], recv_sem=s_recv.at[other],
            device_id={"expert": other}, device_id_type=MESH,
        )

    for d in range(1, n):
        stat(d).start()

    def arrived(kind, at):
        return rx[kind, :, :, :, at].astype(F32).reshape(n * CAP, CHUNK).astype(BF16)

    hidden = wg.shape[1]
    zero = jnp.zeros((n * CAP, hidden), F32)

    def gate_up(kind):
        def step(at, carry):
            rows = arrived(kind, at)
            return carry[0] + dot(rows, wg[at, :]), carry[1] + dot(rows, wu[at, :])

        return columns(width, step, (zero, zero))

    relay(0)

    heads[1].wait_recv()

    def gather_grads(at, carry):
        to_slab(1, dot(b_pick, head_in[1, :, at]) * b_gate, at)
        return carry

    columns(width, gather_grads)
    dispatch(1)

    heads[0].wait_recv()

    def gather_fwd(at, total):
        rows = dot(f_pick, head_in[0, :, at])
        wide[:, at] = rows
        return total + jnp.sum(rows * rows, axis=1, keepdims=True)

    square = columns(width, gather_fwd, jnp.zeros((SLOTS, 1), F32))
    fwd_inv = lax.rsqrt(square / width + EPSILON)

    def norm_fwd(at, carry):
        to_slab(2, wide[:, at] * fwd_inv * gain_ref[:, at].astype(F32), at)
        return carry

    columns(width, norm_fwd)
    dispatch(2)
    for copy in tails:
        copy.start()

    loads[8].wait()
    loads[9].wait()
    complete(0)
    gate_b, up_b = gate_up(0)
    sigma = jax.nn.sigmoid(gate_b)
    terms[0] = up_b * sigma * (1.0 + gate_b * (1.0 - sigma))
    terms[1] = gate_b * sigma
    relay(1)
    relay(2)
    loads[10].wait()
    complete(1)

    piece = width // PIECES

    def pair(which, p):
        return pltpu.make_async_remote_copy(
            src_ref=part.at[which, p, 1 - core], dst_ref=pair_in.at[which, p],
            send_sem=p_send.at[which, p], recv_sem=p_recv.at[which, p],
            device_id={"expert": sibling}, device_id_type=MESH,
        )

    def to_home(which, p, d):
        other = peer(d)
        return pltpu.make_async_remote_copy(
            src_ref=summed.at[which, p, other], dst_ref=home.at[which, p, mine],
            send_sem=h_send.at[which, p, other], recv_sem=h_recv.at[which, p, mine],
            device_id={"expert": 2 * other + core}, device_id_type=MESH,
        )

    def from_holder(which, p, d):
        other = peer(d)
        return pltpu.make_async_remote_copy(
            src_ref=summed.at[which, p, other], dst_ref=home.at[which, p, other],
            send_sem=h_send.at[which, p, other], recv_sem=h_recv.at[which, p, other],
            device_id={"expert": 2 * other + core}, device_id_type=MESH,
        )

    def pieces(which, make):
        for p in range(PIECES):
            def fill(i, carry, p=p):
                at = pl.ds(pl.multiple_of(i * CHUNK, CHUNK), CHUNK)
                full = pl.ds(pl.multiple_of(p * piece + i * CHUNK, CHUNK), CHUNK)
                rows = make(full)
                part[which, p, :, :, :, at] = rows.reshape(2, half, CAP, CHUNK).astype(BF16)
                return carry

            lax.fori_loop(0, piece // CHUNK, fill, 0)
            pair(which, p).start()

    def give(which, p):
        pair(which, p).wait_recv()

        def add(at, carry):
            total = part[which, p, core, :, :, at].astype(F32)
            total = total + pair_in[which, p, :, :, at].astype(F32)
            summed[which, p, :, :, at] = total.astype(BF16)
            return carry

        columns(piece, add)
        for d in range(1, half):
            to_home(which, p, d).start()
        home[which, p, mine] = summed[which, p, mine]

    d_hidden = columns(
        width,
        lambda at, total: total
        + lax.dot_general(arrived(1, at), wd[:, at], NT, preferred_element_type=F32),
        zero,
    )
    d_gate = (d_hidden * terms[0]).astype(BF16)
    d_up = (d_hidden * terms[1]).astype(BF16)

    def input_grad(at):
        rows = lax.dot_general(d_gate, wg[at, :], NT, preferred_element_type=F32)
        return rows + lax.dot_general(d_up, wu[at, :], NT, preferred_element_type=F32)

    pieces(0, input_grad)
    complete(2)
    for p in range(PIECES):
        give(0, p)
    gate_f, up_f = gate_up(2)
    hidden_rows = (gate_f * jax.nn.sigmoid(gate_f) * up_f).astype(BF16)
    pieces(1, lambda at: dot(hidden_rows, wd[:, at]))
    for p in range(PIECES):
        give(1, p)

    for d in range(1, n):
        stat_arrival(d).wait_recv()
    counts = stats[0]
    for i in range(1, n):
        counts = counts + stats[i]
    tokens_all = tokens * n
    balance_ref[...] = (
        EXPERTS * (counts[0:1] / (tokens_all * TOPK)) * (counts[1:2] / tokens_all)
    )

    def returned(which, p, at):
        rows = []
        for e in range(EXP_WIN):
            total = home[which, p, e * span, :, at].astype(F32)
            for i in range(1, span):
                total = total + home[which, p, e * span + i, :, at].astype(F32)
            rows.append(total)
        return jnp.concatenate(rows, axis=0)

    def by_piece(which, p, step, init):
        for d in range(1, half):
            from_holder(which, p, d).wait_recv()

        def run(i, carry):
            at = pl.ds(pl.multiple_of(i * CHUNK, CHUNK), CHUNK)
            full = pl.ds(pl.multiple_of(p * piece + i * CHUNK, CHUNK), CHUNK)
            return step(full, returned(which, p, at), carry)

        return lax.fori_loop(0, piece // CHUNK, run, init)

    def combine(back, which, rows, at):
        high, low = halves(rows)
        stack = jnp.concatenate([head_in[which, :, at], tail_in[which, :, at], high, low], axis=0)
        return dot(back, stack).astype(BF16)

    def weigh(at, rows, total):
        weighted = rows * gain_ref[:, at].astype(F32)
        wide[:, at] = weighted
        return total + jnp.sum(weighted * raw[:, at], axis=1, keepdims=True)

    total = jnp.zeros((SLOTS, 1), F32)
    for p in range(PIECES):
        total = by_piece(0, p, weigh, total)
    scale = saved_inv * saved_inv * saved_inv * (total / width)
    tails[1].wait_recv()

    def finish_bwd(at, carry):
        rows = saved_inv * wide[:, at] - raw[:, at] * scale
        bout_ref[:, at] = combine(b_back, 1, rows, at)
        return carry

    columns(width, finish_bwd)
    tails[0].wait_recv()

    def finish_fwd(at, rows, carry):
        fout_ref[:, at] = combine(f_back, 0, rows * f_gate, at)
        return carry

    for p in range(PIECES):
        by_piece(1, p, finish_fwd, 0)

    for copy in places + heads + tails:
        copy.wait_send()
    for kind in range(3):
        for d in range(half):
            forward(kind, core, peer(d)).wait_send()
        for d in range(1, half):
            direct(kind, d).wait_send()
    for which in range(2):
        for p in range(PIECES):
            pair(which, p).wait_send()
            for d in range(1, half):
                to_home(which, p, d).wait_send()
    for d in range(1, n):
        stat(d).wait_send()


def body(
    sections, n,
    fwd_sent, bwd_sent, bwd_saved, fwd_routes, bwd_routes, fwd_logits, bwd_logits,
    norm_gain, w_gate, w_up, w_down,
):
    tokens, width = fwd_sent.shape[1:]
    hidden = w_gate.shape[2]
    half = n // 2
    vmem = pl.BlockSpec(memory_space=pltpu.VMEM)
    hbm = pl.BlockSpec(memory_space=pl.ANY)
    dma = pltpu.SemaphoreType.DMA
    fwd_out, bwd_out, balance = pl.pallas_call(
        functools.partial(kernel, sections, n),
        out_shape=(
            jax.ShapeDtypeStruct((tokens, width), BF16),
            jax.ShapeDtypeStruct((tokens, width), BF16),
            jax.ShapeDtypeStruct((1, EXPERTS), F32),
        ),
        in_specs=[hbm] * 11,
        out_specs=(vmem, vmem, vmem),
        scratch_shapes=[
            pltpu.VMEM((TOPK, tokens), jnp.int32),
            pltpu.VMEM((TOPK, tokens), jnp.int32),
            pltpu.VMEM((tokens, EXPERTS), F32),
            pltpu.VMEM((tokens, EXPERTS), F32),
            pltpu.VMEM((tokens, width), BF16),
            pltpu.VMEM((tokens, width), BF16),
            pltpu.VMEM((tokens, width), BF16),
            pltpu.VMEM((1, width), BF16),
            pltpu.VMEM((width, hidden), BF16),
            pltpu.VMEM((width, hidden), BF16),
            pltpu.VMEM((hidden, width), BF16),
            pltpu.VMEM((2, 8, tokens), F32),
            pltpu.VMEM((2, 8, tokens), F32),
            pltpu.VMEM((2, HEAD, width), BF16),
            pltpu.VMEM((2, tokens - HEAD, width), BF16),
            pltpu.VMEM((2, HEAD, width), BF16),
            pltpu.VMEM((2, tokens - HEAD, width), BF16),
            pltpu.VMEM((3, EXP_WIN, CAP, width), BF16),
            pltpu.VMEM((3, 2, half, CAP, width), BF16),
            pltpu.VMEM((2, PIECES, 2, half, CAP, width // PIECES), BF16),
            pltpu.VMEM((2, PIECES, half, CAP, width // PIECES), BF16),
            pltpu.VMEM((2, PIECES, half, CAP, width // PIECES), BF16),
            pltpu.VMEM((2, PIECES, half, CAP, width // PIECES), BF16),
            pltpu.VMEM((SLOTS, width), F32),
            pltpu.VMEM((SLOTS, width), F32),
            pltpu.VMEM((2, n * CAP, hidden), F32),
            pltpu.VMEM((n, 8, EXPERTS), F32),
            dma((11,)), dma((6,)), dma((6,)),
            dma((3, half)), dma((3, half)), dma((3, half)), dma((3, half)),
            dma((2, PIECES)), dma((2, PIECES)), dma((2, PIECES, half)), dma((2, PIECES, half)),
            dma((n,)), dma((n,)),
        ],
        compiler_params=pltpu.CompilerParams(
            collective_id=0, has_side_effects=True, vmem_limit_bytes=60 * 1024 * 1024
        ),
    )(
        fwd_routes[0].T, bwd_routes[0].T, fwd_logits[0], bwd_logits[0],
        fwd_sent[0], bwd_sent[0], bwd_saved[0], norm_gain, w_gate[0], w_up[0], w_down[0],
    )
    return fwd_out[None], bwd_out[None], balance


def solution(mesh):
    block = P("section", "expert", None)
    return jax.shard_map(
        functools.partial(body, mesh.shape["section"], mesh.shape["expert"]),
        mesh=mesh,
        in_specs=(block,) * 7
        + (
            P("section", None),
            P("section", None, "expert"),
            P("section", None, "expert"),
            P("section", "expert", None),
        ),
        out_specs=(block, block, P("section", None)),
        check_vma=False,
    )
```

```python
import functools

import jax
import jax.numpy as jnp
from jax import lax
from jax.experimental import pallas as pl
from jax.experimental.pallas import tpu as pltpu
from jax.sharding import PartitionSpec as P

EXPERTS = 128
TOPK = 8
EXP_WIN = 2
CAP = 8
SLOTS = EXP_WIN * CAP
HEAD = 16
CHUNK = 1024
WIDE = 2048
PIECES = 2
EPSILON = 1e-06
MESH = pl.DeviceIdType.MESH
F32 = jnp.float32
BF16 = jnp.bfloat16
NT = (((1,), (1,)), ((), ()))


def iota(shape, dim):
    return lax.broadcasted_iota(jnp.int32, shape, dim)


def dot(a, b):
    return jnp.dot(a, b, preferred_element_type=F32)


def columns(width, body, init=0, chunk=1024):
    if chunk >= width:
        return body(pl.ds(0, width), init)

    def step(i, carry):
        return body(pl.ds(pl.multiple_of(i * chunk, chunk), chunk), carry)

    return lax.fori_loop(0, width // chunk, step, init)


def route_tables(routes, logits):
    tokens, experts = logits.shape
    lane = iota((tokens, experts), 1)
    unit = (iota((tokens, tokens), 0) == iota((tokens, tokens), 1)).astype(BF16)
    routes = lax.dot_general(
        unit, routes.astype(F32).astype(BF16), NT, preferred_element_type=F32
    )
    chosen = routes[:, 0:1] == lane.astype(F32)
    for k in range(1, TOPK):
        chosen = chosen | (routes[:, k : k + 1] == lane.astype(F32))
    hit = chosen.astype(F32)
    top = jnp.max(jnp.where(chosen, logits, -jnp.inf), axis=1, keepdims=True)
    raised = jnp.exp(jnp.where(chosen, logits, top) - top) * hit
    gates = raised / jnp.sum(raised, axis=1, keepdims=True)
    here = jnp.max(jnp.where(lane < EXP_WIN, hit, 0.0), axis=1, keepdims=True)
    marks = jnp.where(lane < EXP_WIN, hit, jnp.where(lane == EXP_WIN, here, 0.0))
    below = (iota((tokens, tokens), 1) < iota((tokens, tokens), 0)).astype(BF16)
    earlier = dot(below, marks.astype(BF16))
    before = earlier[:, EXP_WIN : EXP_WIN + 1]
    count = jnp.sum(here, axis=0, keepdims=True)
    place = jnp.where(
        here > 0.0, before, count + iota((tokens, 1), 0).astype(F32) - before
    )

    def slot_at(slot):
        taken = jnp.zeros(slot.shape, F32)
        gated = jnp.zeros(slot.shape, F32)
        for e in range(EXP_WIN):
            there = (slot // CAP == e) & (
                earlier[:, e : e + 1] == (slot - e * CAP).astype(F32)
            )
            mine = jnp.where(there, hit[:, e : e + 1], 0.0)
            taken = taken + mine
            gated = gated + mine * gates[:, e : e + 1]
        return taken, gated

    taken, gated = slot_at(lane)
    taken = jnp.where(lane < SLOTS, taken, 0.0)
    gated = jnp.where(lane < SLOTS, gated, 0.0)
    turned = jnp.concatenate([taken, gated], axis=0).T
    select = turned[:SLOTS, :tokens].astype(BF16)
    right = iota((SLOTS, 2 * tokens), 1) >= tokens
    gate_slot = jnp.sum(jnp.where(right, turned[:SLOTS], 0.0), axis=1, keepdims=True)
    again = lane - tokens
    again = jnp.where(again >= SLOTS, again - SLOTS, again)
    back = jnp.where(
        lane < tokens,
        (place == lane.astype(F32)).astype(F32),
        jnp.where(lane < tokens + 2 * SLOTS, slot_at(again)[0], 0.0),
    ).astype(BF16)
    head_select = dot(select, back[:, :HEAD]).astype(BF16)
    return hit, select, head_select, gate_slot, back


def place_row(routes):
    tokens = routes.shape[1]
    here = jnp.max(jnp.where(routes < EXP_WIN, 1.0, 0.0), axis=0, keepdims=True)
    here = jnp.broadcast_to(here, (8, tokens))
    above = (iota((tokens, tokens), 0) < iota((tokens, tokens), 1)).astype(BF16)
    before = dot(here.astype(BF16), above)
    count = jnp.sum(here, axis=1, keepdims=True)
    order = iota((8, tokens), 1).astype(F32)
    return jnp.where(here > 0.0, before, count + order - before)


def permutation(place, tokens):
    return (iota((tokens, tokens), 0).astype(F32) == place).astype(BF16)


def halves(rows):
    high = rows.astype(BF16)
    low = (rows - high.astype(F32)).astype(BF16)
    return jnp.concatenate([high, low], axis=0)


def kernel(
    sections, n,
    froute_hbm, broute_hbm, flogit_hbm, blogit_hbm, fwd_hbm, bwd_hbm, saved_hbm, gain_hbm,
    wg_hbm, wu_hbm, wd_hbm,
    stack_hbm, back_hbm, balance_hbm,
    froute_ref, broute_ref, flogit_ref, blogit_ref, fwd_ref, bwd_ref, saved_ref, gain_ref,
    wgu, wd, place_out, place_in, head_out, tail_out, head_in,
    halved, back_ref, balance_ref,
    slab, rx, part, pair_in, summed, home, raw, wide, terms, stats,
    w_sem, o_sem, z_send, z_recv, d_send, d_recv, f_send, f_recv,
    p_send, p_recv, h_send, h_recv, s_send, s_recv,
):
    tokens, width = fwd_ref.shape
    hidden = wd.shape[0]
    half = n // 2
    span = half // EXP_WIN
    sec, me = lax.axis_index("section"), lax.axis_index("expert")
    core, mine = lax.rem(me, 2), me // 2
    sibling = me + 1 - 2 * core
    after, ahead = lax.rem(sec + 1, sections), lax.rem(sec + sections - 1, sections)

    joined = wgu.shape[0] == 1
    if joined:
        gate_side, up_side = (wgu.at[0, :, pl.ds(i * hidden, hidden)] for i in range(2))
    else:
        gate_side, up_side = wgu.at[0], wgu.at[1]
    loads = [
        pltpu.make_async_copy(src, dst, w_sem.at[i])
        for i, (src, dst) in enumerate((
            (froute_hbm, froute_ref), (broute_hbm, broute_ref),
            (flogit_hbm, flogit_ref), (blogit_hbm, blogit_ref),
            (fwd_hbm, fwd_ref), (bwd_hbm, bwd_ref), (saved_hbm, saved_ref), (gain_hbm, gain_ref),
            (wg_hbm, gate_side), (wu_hbm, up_side), (wd_hbm, wd),
        ))
    ]
    for load in loads:
        load.start()

    barrier = pltpu.get_barrier_semaphore()
    for d in range(1, n):
        pl.semaphore_signal(
            barrier, inc=1, device_id={"expert": lax.rem(me + d, n)}, device_id_type=MESH
        )
    for where in (after, ahead):
        pl.semaphore_signal(barrier, inc=1, device_id={"section": where}, device_id_type=MESH)

    loads[0].wait()
    loads[1].wait()
    place_out[0] = place_row(froute_ref[...])
    place_out[1] = place_row(broute_ref[...])
    pl.semaphore_wait(barrier, n + 1)

    def z_copy(which, src, dst, where):
        return pltpu.make_async_remote_copy(
            src_ref=src, dst_ref=dst, send_sem=z_send.at[which], recv_sem=z_recv.at[which],
            device_id={"section": where}, device_id_type=MESH,
        )

    places = [
        z_copy(0, place_out.at[0], place_in.at[0], ahead),
        z_copy(1, place_out.at[1], place_in.at[1], after),
    ]
    heads = [
        z_copy(2, head_out.at[0], head_in.at[0], after),
        z_copy(3, head_out.at[1], head_in.at[1], ahead),
    ]
    tails = [
        z_copy(4, tail_out.at[0], stack_hbm.at[0, pl.ds(HEAD, tokens - HEAD)], after),
        z_copy(5, tail_out.at[1], stack_hbm.at[1, pl.ds(HEAD, tokens - HEAD)], ahead),
    ]
    head_keep = [
        pltpu.make_async_copy(head_in.at[i], stack_hbm.at[i, pl.ds(0, HEAD)], o_sem.at[i])
        for i in range(2)
    ]
    for copy in places:
        copy.start()

    loads[2].wait()
    loads[3].wait()
    hit, _, f_pick, f_gate, f_back = route_tables(froute_ref[...], flogit_ref[...])
    _, b_select, b_pick, b_gate, b_back = route_tables(broute_ref[...], blogit_ref[...])

    back_ref[0] = f_back
    back_ref[1] = b_back
    back_keep = pltpu.make_async_copy(back_ref, back_hbm, o_sem.at[2])
    back_keep.start()

    def peer(d):
        return lax.rem(mine + d, half)

    def direct(kind, d):
        other = peer(d)
        return pltpu.make_async_remote_copy(
            src_ref=slab.at[kind, other // span], dst_ref=rx.at[kind, core, mine],
            send_sem=d_send.at[kind, other], recv_sem=d_recv.at[kind, mine],
            device_id={"expert": 2 * other + core}, device_id_type=MESH,
        )

    def arrival(kind, d):
        other = peer(d)
        return pltpu.make_async_remote_copy(
            src_ref=slab.at[kind, 0], dst_ref=rx.at[kind, core, other],
            send_sem=d_send.at[kind, other], recv_sem=d_recv.at[kind, other],
            device_id={"expert": 2 * other + core}, device_id_type=MESH,
        )

    def forward(kind, side, other):
        return pltpu.make_async_remote_copy(
            src_ref=rx.at[kind, side, other], dst_ref=rx.at[kind, side, other],
            send_sem=f_send.at[kind, other], recv_sem=f_recv.at[kind, other],
            device_id={"expert": sibling}, device_id_type=MESH,
        )

    def dispatch(kind):
        for d in range(1, half):
            direct(kind, d).start()
        rx[kind, core, mine] = slab[kind, mine // span]
        forward(kind, core, mine).start()

    def relay(kind):
        for d in range(1, half):
            arrival(kind, d).wait_recv()
            forward(kind, core, peer(d)).start()

    def complete(kind):
        for d in range(half):
            forward(kind, 1 - core, peer(d)).wait_recv()

    def to_slab(kind, rows, at):
        for e in range(EXP_WIN):
            slab[kind, e, :, at] = rows[e * CAP : (e + 1) * CAP].astype(BF16)

    loads[4].wait()
    loads[5].wait()
    sources = (fwd_ref, bwd_ref)
    orders = []
    for which in range(2):
        places[which].wait_recv()
        orders.append(permutation(place_in[which, 0:1], tokens))

    for which in range(2):
        def fill_head(at, carry, which=which):
            head_out[which, :, at] = dot(orders[which][:HEAD], sources[which][:, at]).astype(BF16)
            return carry

        columns(width, fill_head, chunk=WIDE)
        heads[which].start()

    loads[6].wait()
    loads[7].wait()

    def gather_saved(at, total):
        rows = dot(b_select, saved_ref[:, at])
        raw[:, at] = rows
        return total + jnp.sum(rows * rows, axis=1, keepdims=True)

    square = columns(width, gather_saved, jnp.zeros((SLOTS, 1), F32), chunk=WIDE)
    saved_inv = lax.rsqrt(square / width + EPSILON)

    def norm_saved(at, carry):
        to_slab(0, raw[:, at] * saved_inv * gain_ref[:, at].astype(F32), at)
        return carry

    columns(width, norm_saved, chunk=WIDE)
    dispatch(0)

    for which in range(2):
        def fill_tail(at, carry, which=which):
            tail_out[which, :, at] = dot(orders[which][HEAD:], sources[which][:, at]).astype(BF16)
            return carry

        columns(width, fill_tail)

    logits = flogit_ref[...]
    raised = jnp.exp(logits - jnp.max(logits, axis=1, keepdims=True))
    probs = raised / jnp.sum(raised, axis=1, keepdims=True)
    count_row = jnp.sum(hit, axis=0, keepdims=True)
    prob_row = jnp.sum(probs, axis=0, keepdims=True)
    row = iota((8, EXPERTS), 0)
    stats[me] = jnp.where(row == 0, count_row, jnp.where(row == 1, prob_row, 0.0))

    def stat(d):
        other = lax.rem(me + d, n)
        return pltpu.make_async_remote_copy(
            src_ref=stats.at[me], dst_ref=stats.at[me],
            send_sem=s_send.at[other], recv_sem=s_recv.at[me],
            device_id={"expert": other}, device_id_type=MESH,
        )

    def stat_arrival(d):
        other = lax.rem(me + d, n)
        return pltpu.make_async_remote_copy(
            src_ref=stats.at[other], dst_ref=stats.at[other],
            send_sem=s_send.at[other], recv_sem=s_recv.at[other],
            device_id={"expert": other}, device_id_type=MESH,
        )

    for d in range(1, n):
        stat(d).start()

    def arrived(kind, at):
        return rx[kind, :, :, :, at].astype(F32).reshape(n * CAP, CHUNK).astype(BF16)

    zero = jnp.zeros((n * CAP, hidden), F32)

    def gate_up(kind):
        def step(at, totals):
            rows = arrived(kind, at)
            return tuple(total + dot(rows, wgu[i, at, :]) for i, total in enumerate(totals))

        empty = jnp.zeros((n * CAP, wgu.shape[2]), F32)
        totals = columns(width, step, (empty,) * wgu.shape[0])
        return (totals[0][:, :hidden], totals[0][:, hidden:]) if joined else totals

    relay(0)

    heads[1].wait_recv()
    heads[0].wait_recv()
    for copy in tails:
        copy.start()
    for copy in head_keep:
        copy.start()


    def gather_grads(at, carry):
        to_slab(1, dot(b_pick, head_in[1, :, at]) * b_gate, at)
        return carry

    columns(width, gather_grads, chunk=WIDE)
    dispatch(1)


    def gather_fwd(at, total):
        rows = dot(f_pick, head_in[0, :, at])
        wide[:, at] = rows
        return total + jnp.sum(rows * rows, axis=1, keepdims=True)

    square = columns(width, gather_fwd, jnp.zeros((SLOTS, 1), F32), chunk=WIDE)
    fwd_inv = lax.rsqrt(square / width + EPSILON)

    def norm_fwd(at, carry):
        to_slab(2, wide[:, at] * fwd_inv * gain_ref[:, at].astype(F32), at)
        return carry

    columns(width, norm_fwd, chunk=WIDE)
    dispatch(2)

    loads[8].wait()
    loads[9].wait()
    complete(0)
    gate_b, up_b = gate_up(0)
    sigma = jax.nn.sigmoid(gate_b)
    terms[0] = up_b * sigma * (1.0 + gate_b * (1.0 - sigma))
    terms[1] = gate_b * sigma
    relay(1)
    relay(2)
    loads[10].wait()
    complete(1)

    piece = width // PIECES

    def pair(which, p):
        return pltpu.make_async_remote_copy(
            src_ref=part.at[which, p, 1 - core], dst_ref=pair_in.at[which, p],
            send_sem=p_send.at[which, p], recv_sem=p_recv.at[which, p],
            device_id={"expert": sibling}, device_id_type=MESH,
        )

    def to_home(which, p, d):
        other = peer(d)
        return pltpu.make_async_remote_copy(
            src_ref=summed.at[which, p, other], dst_ref=home.at[which, p, mine],
            send_sem=h_send.at[which, p, other], recv_sem=h_recv.at[which, p, mine],
            device_id={"expert": 2 * other + core}, device_id_type=MESH,
        )

    def from_holder(which, p, d):
        other = peer(d)
        return pltpu.make_async_remote_copy(
            src_ref=summed.at[which, p, other], dst_ref=home.at[which, p, other],
            send_sem=h_send.at[which, p, other], recv_sem=h_recv.at[which, p, other],
            device_id={"expert": 2 * other + core}, device_id_type=MESH,
        )

    def pieces(which, make):
        for p in range(PIECES):
            def fill(i, carry, p=p):
                at = pl.ds(pl.multiple_of(i * CHUNK, CHUNK), CHUNK)
                full = pl.ds(pl.multiple_of(p * piece + i * CHUNK, CHUNK), CHUNK)
                rows = make(full)
                part[which, p, :, :, :, at] = rows.reshape(2, half, CAP, CHUNK).astype(BF16)
                return carry

            lax.fori_loop(0, piece // CHUNK, fill, 0)
            pair(which, p).start()

    def give(which, p):
        pair(which, p).wait_recv()

        def add(at, carry):
            total = part[which, p, core, :, :, at].astype(F32)
            total = total + pair_in[which, p, :, :, at].astype(F32)
            summed[which, p, :, :, at] = total.astype(BF16)
            return carry

        columns(piece, add)
        for d in range(1, half):
            to_home(which, p, d).start()
        home[which, p, mine] = summed[which, p, mine]

    d_hidden = columns(
        width,
        lambda at, total: total
        + lax.dot_general(arrived(1, at), wd[:, at], NT, preferred_element_type=F32),
        zero,
    )
    d_parts = [(d_hidden * terms[i]).astype(BF16) for i in range(2)]
    if joined:
        d_parts = [jnp.concatenate(d_parts, axis=1)]

    def input_grad(at):
        return sum(
            lax.dot_general(d_part, wgu[i, at, :], NT, preferred_element_type=F32)
            for i, d_part in enumerate(d_parts)
        )

    pieces(0, input_grad)
    complete(2)
    give(0, 0)
    gate_f, up_f = gate_up(2)
    hidden_rows = (gate_f * jax.nn.sigmoid(gate_f) * up_f).astype(BF16)
    for p in range(1, PIECES):
        give(0, p)
    pieces(1, lambda at: dot(hidden_rows, wd[:, at]))
    for p in range(PIECES):
        give(1, p)

    for d in range(1, n):
        stat_arrival(d).wait_recv()
    counts = stats[0]
    for i in range(1, n):
        counts = counts + stats[i]
    tokens_all = tokens * n
    balance_ref[...] = (
        EXPERTS * (counts[0:1] / (tokens_all * TOPK)) * (counts[1:2] / tokens_all)
    )
    balance_keep = pltpu.make_async_copy(balance_ref, balance_hbm, o_sem.at[3])
    balance_keep.start()

    def returned(which, p, at):
        rows = []
        for e in range(EXP_WIN):
            total = home[which, p, e * span, :, at].astype(F32)
            for i in range(1, span):
                total = total + home[which, p, e * span + i, :, at].astype(F32)
            rows.append(total)
        return jnp.concatenate(rows, axis=0)

    def by_piece(which, p, step, init):
        for d in range(1, half):
            from_holder(which, p, d).wait_recv()

        def run(i, carry):
            at = pl.ds(pl.multiple_of(i * CHUNK, CHUNK), CHUNK)
            full = pl.ds(pl.multiple_of(p * piece + i * CHUNK, CHUNK), CHUNK)
            return step(full, returned(which, p, at), carry)

        return lax.fori_loop(0, piece // CHUNK, run, init)

    def weigh(at, rows, total):
        weighted = rows * gain_ref[:, at].astype(F32)
        wide[:, at] = weighted
        return total + jnp.sum(weighted * raw[:, at], axis=1, keepdims=True)

    total = jnp.zeros((SLOTS, 1), F32)
    for p in range(PIECES):
        total = by_piece(0, p, weigh, total)
    scale = saved_inv * saved_inv * saved_inv * (total / width)

    def rows_copy(which, at, i):
        rows = pl.ds(tokens, 2 * SLOTS)
        return pltpu.make_async_copy(
            halved.at[which, :, at], stack_hbm.at[which, rows, at], o_sem.at[4 + i]
        )

    def finish_bwd(at, carry):
        rows = saved_inv * wide[:, at] - raw[:, at] * scale
        halved[1, :, at] = halves(rows)
        return carry

    columns(width, finish_bwd, chunk=WIDE)
    kept = [rows_copy(1, pl.ds(0, width), PIECES)]
    kept[0].start()

    def finish_fwd(at, rows, carry):
        halved[0, :, at] = halves(rows * f_gate)
        return carry

    for p in range(PIECES):
        by_piece(1, p, finish_fwd, 0)
        kept.append(rows_copy(0, pl.ds(p * piece, piece), p))
        kept[-1].start()

    for copy in tails:
        copy.wait_recv()
    for copy in head_keep + [back_keep, balance_keep] + kept:
        copy.wait()
    for copy in places + heads + tails:
        copy.wait_send()
    for kind in range(3):
        for d in range(half):
            forward(kind, core, peer(d)).wait_send()
        for d in range(1, half):
            direct(kind, d).wait_send()
    for which in range(2):
        for p in range(PIECES):
            pair(which, p).wait_send()
            for d in range(1, half):
                to_home(which, p, d).wait_send()
    for d in range(1, n):
        stat(d).wait_send()


def place_kernel(
    stack_hbm, back_hbm, balance_hbm, fout_hbm, bout_hbm, out_hbm,
    stack, back, balance, out, in_sem, out_sem, small_sem,
):
    _, rows, width = stack.shape
    steps = width // CHUNK
    spans = [pl.ds(i * CHUNK, CHUNK) for i in range(steps)]
    small = [
        pltpu.make_async_copy(back_hbm, back, small_sem.at[0]),
        pltpu.make_async_copy(balance_hbm, balance, small_sem.at[1]),
    ]
    loads = [
        pltpu.make_async_copy(stack_hbm.at[:, :, at], stack.at[:, :, at], in_sem.at[i])
        for i, at in enumerate(spans)
    ]
    for copy in small + loads:
        copy.start()
    small[1].wait()
    last = pltpu.make_async_copy(balance, out_hbm, small_sem.at[2])
    last.start()
    small[0].wait()
    stores = []
    for i, at in enumerate(spans):
        loads[i].wait()
        for which, target in enumerate((fout_hbm, bout_hbm)):
            out[which, :, at] = dot(back[which, :, :rows], stack[which, :, at]).astype(BF16)
            store = pltpu.make_async_copy(
                out.at[which, :, at], target.at[:, at], out_sem.at[which, i]
            )
            store.start()
            stores.append(store)
    for copy in stores + [last]:
        copy.wait()


def body(
    sections, n,
    fwd_sent, bwd_sent, bwd_saved, fwd_routes, bwd_routes, fwd_logits, bwd_logits,
    norm_gain, w_gate, w_up, w_down,
):
    tokens, width = fwd_sent.shape[1:]
    hidden = w_gate.shape[2]
    half = n // 2
    hbm = pl.BlockSpec(memory_space=pl.ANY)
    dma = pltpu.SemaphoreType.DMA
    rows = tokens + 2 * SLOTS
    stack, back, balance = pl.pallas_call(
        functools.partial(kernel, sections, n),
        out_shape=(
            jax.ShapeDtypeStruct((2, rows, width), BF16),
            jax.ShapeDtypeStruct((2, tokens, EXPERTS), BF16),
            jax.ShapeDtypeStruct((1, EXPERTS), F32),
        ),
        in_specs=[hbm] * 11,
        out_specs=(hbm, hbm, hbm),
        scratch_shapes=[
            pltpu.VMEM((TOPK, tokens), jnp.int32),
            pltpu.VMEM((TOPK, tokens), jnp.int32),
            pltpu.VMEM((tokens, EXPERTS), F32),
            pltpu.VMEM((tokens, EXPERTS), F32),
            pltpu.VMEM((tokens, width), BF16),
            pltpu.VMEM((tokens, width), BF16),
            pltpu.VMEM((tokens, width), BF16),
            pltpu.VMEM((1, width), BF16),
            pltpu.VMEM((1, width, 2 * hidden) if hidden % 128 == 0 else (2, width, hidden), BF16),
            pltpu.VMEM((hidden, width), BF16),
            pltpu.VMEM((2, 8, tokens), F32),
            pltpu.VMEM((2, 8, tokens), F32),
            pltpu.VMEM((2, HEAD, width), BF16),
            pltpu.VMEM((2, tokens - HEAD, width), BF16),
            pltpu.VMEM((2, HEAD, width), BF16),
            pltpu.VMEM((2, 2 * SLOTS, width), BF16),
            pltpu.VMEM((2, tokens, EXPERTS), BF16),
            pltpu.VMEM((1, EXPERTS), F32),
            pltpu.VMEM((3, EXP_WIN, CAP, width), BF16),
            pltpu.VMEM((3, 2, half, CAP, width), BF16),
            pltpu.VMEM((2, PIECES, 2, half, CAP, width // PIECES), BF16),
            pltpu.VMEM((2, PIECES, half, CAP, width // PIECES), BF16),
            pltpu.VMEM((2, PIECES, half, CAP, width // PIECES), BF16),
            pltpu.VMEM((2, PIECES, half, CAP, width // PIECES), BF16),
            pltpu.VMEM((SLOTS, width), F32),
            pltpu.VMEM((SLOTS, width), F32),
            pltpu.VMEM((2, n * CAP, hidden), F32),
            pltpu.VMEM((n, 8, EXPERTS), F32),
            dma((11,)), dma((5 + PIECES,)), dma((6,)), dma((6,)),
            dma((3, half)), dma((3, half)), dma((3, half)), dma((3, half)),
            dma((2, PIECES)), dma((2, PIECES)), dma((2, PIECES, half)), dma((2, PIECES, half)),
            dma((n,)), dma((n,)),
        ],
        compiler_params=pltpu.CompilerParams(
            collective_id=0, has_side_effects=True, vmem_limit_bytes=60 * 1024 * 1024
        ),
    )(
        fwd_routes[0].T, bwd_routes[0].T, fwd_logits[0], bwd_logits[0],
        fwd_sent[0], bwd_sent[0], bwd_saved[0], norm_gain, w_gate[0], w_up[0], w_down[0],
    )
    fwd_out, bwd_out, balance = pl.pallas_call(
        place_kernel,
        out_shape=(
            jax.ShapeDtypeStruct((tokens, width), BF16),
            jax.ShapeDtypeStruct((tokens, width), BF16),
            jax.ShapeDtypeStruct((1, EXPERTS), F32),
        ),
        in_specs=[hbm] * 3,
        out_specs=(hbm, hbm, hbm),
        scratch_shapes=[
            pltpu.VMEM((2, rows, width), BF16),
            pltpu.VMEM((2, tokens, EXPERTS), BF16),
            pltpu.VMEM((1, EXPERTS), F32),
            pltpu.VMEM((2, tokens, width), BF16),
            dma((width // CHUNK,)), dma((2, width // CHUNK)), dma((3,)),
        ],
        compiler_params=pltpu.CompilerParams(vmem_limit_bytes=60 * 1024 * 1024),
    )(stack, back, balance)
    return fwd_out[None], bwd_out[None], balance


def solution(mesh):
    block = P("section", "expert", None)
    return jax.shard_map(
        functools.partial(body, mesh.shape["section"], mesh.shape["expert"]),
        mesh=mesh,
        in_specs=(block,) * 7
        + (
            P("section", None),
            P("section", None, "expert"),
            P("section", None, "expert"),
            P("section", "expert", None),
        ),
        out_specs=(block, block, P("section", None)),
        check_vma=False,
    )
```

```python
import functools

import jax
import jax.numpy as jnp
from jax import lax
from jax.experimental import pallas as pl
from jax.experimental.pallas import tpu as pltpu
from jax.sharding import PartitionSpec as P

EXPERTS = 128
TOPK = 8
EXP_WIN = 2
CAP = 8
SLOTS = EXP_WIN * CAP
HEAD = 16
CHUNK = 1024
WIDE = 2048
PIECES = 4
EPSILON = 1e-06
MESH = pl.DeviceIdType.MESH
F32 = jnp.float32
BF16 = jnp.bfloat16
NT = (((1,), (1,)), ((), ()))


def iota(shape, dim):
    return lax.broadcasted_iota(jnp.int32, shape, dim)


def dot(a, b):
    return jnp.dot(a, b, preferred_element_type=F32)


def columns(width, body, init=0, chunk=1024):
    if chunk >= width:
        return body(pl.ds(0, width), init)

    def step(i, carry):
        return body(pl.ds(pl.multiple_of(i * chunk, chunk), chunk), carry)

    return lax.fori_loop(0, width // chunk, step, init)


def route_tables(routes, logits):
    tokens, experts = logits.shape
    lane = iota((tokens, experts), 1)
    unit = (iota((tokens, tokens), 0) == iota((tokens, tokens), 1)).astype(BF16)
    routes = lax.dot_general(
        unit, routes.astype(F32).astype(BF16), NT, preferred_element_type=F32
    )
    chosen = routes[:, 0:1] == lane.astype(F32)
    for k in range(1, TOPK):
        chosen = chosen | (routes[:, k : k + 1] == lane.astype(F32))
    hit = chosen.astype(F32)
    top = jnp.max(jnp.where(chosen, logits, -jnp.inf), axis=1, keepdims=True)
    raised = jnp.exp(jnp.where(chosen, logits, top) - top) * hit
    gates = raised / jnp.sum(raised, axis=1, keepdims=True)
    here = jnp.max(jnp.where(lane < EXP_WIN, hit, 0.0), axis=1, keepdims=True)
    marks = jnp.where(lane < EXP_WIN, hit, jnp.where(lane == EXP_WIN, here, 0.0))
    below = (iota((tokens, tokens), 1) < iota((tokens, tokens), 0)).astype(BF16)
    earlier = dot(below, marks.astype(BF16))
    before = earlier[:, EXP_WIN : EXP_WIN + 1]
    count = jnp.sum(here, axis=0, keepdims=True)
    place = jnp.where(
        here > 0.0, before, count + iota((tokens, 1), 0).astype(F32) - before
    )

    def slot_at(slot):
        taken = jnp.zeros(slot.shape, F32)
        gated = jnp.zeros(slot.shape, F32)
        for e in range(EXP_WIN):
            there = (slot // CAP == e) & (
                earlier[:, e : e + 1] == (slot - e * CAP).astype(F32)
            )
            mine = jnp.where(there, hit[:, e : e + 1], 0.0)
            taken = taken + mine
            gated = gated + mine * gates[:, e : e + 1]
        return taken, gated

    taken, gated = slot_at(lane)
    taken = jnp.where(lane < SLOTS, taken, 0.0)
    gated = jnp.where(lane < SLOTS, gated, 0.0)
    turned = jnp.concatenate([taken, gated], axis=0).T
    select = turned[:SLOTS, :tokens].astype(BF16)
    right = iota((SLOTS, 2 * tokens), 1) >= tokens
    gate_slot = jnp.sum(jnp.where(right, turned[:SLOTS], 0.0), axis=1, keepdims=True)
    again = lane - tokens
    again = jnp.where(again >= SLOTS, again - SLOTS, again)
    back = jnp.where(
        lane < tokens,
        (place == lane.astype(F32)).astype(F32),
        jnp.where(lane < tokens + 2 * SLOTS, slot_at(again)[0], 0.0),
    ).astype(BF16)
    head_select = dot(select, back[:, :HEAD]).astype(BF16)
    return hit, select, head_select, gate_slot, back


def place_row(routes):
    tokens = routes.shape[1]
    here = jnp.max(jnp.where(routes < EXP_WIN, 1.0, 0.0), axis=0, keepdims=True)
    here = jnp.broadcast_to(here, (8, tokens))
    above = (iota((tokens, tokens), 0) < iota((tokens, tokens), 1)).astype(BF16)
    before = dot(here.astype(BF16), above)
    count = jnp.sum(here, axis=1, keepdims=True)
    order = iota((8, tokens), 1).astype(F32)
    return jnp.where(here > 0.0, before, count + order - before)


def permutation(place, tokens):
    return (iota((tokens, tokens), 0).astype(F32) == place).astype(BF16)


def halves(rows):
    high = rows.astype(BF16)
    low = (rows - high.astype(F32)).astype(BF16)
    return jnp.concatenate([high, low], axis=0)


def kernel(
    sections, n,
    froute_hbm, broute_hbm, flogit_hbm, blogit_hbm, fwd_hbm, bwd_hbm, saved_hbm, gain_hbm,
    wg_hbm, wu_hbm, wd_hbm,
    stack_hbm, back_hbm, balance_hbm,
    froute_ref, broute_ref, flogit_ref, blogit_ref, fwd_ref, bwd_ref, saved_ref, gain_ref,
    wgu, wd, place_out, place_in, head_out, tail_out, head_in,
    halved, back_ref, balance_ref,
    slab, rx, part, pair_in, summed, home, raw, wide, terms, stats,
    w_sem, o_sem, z_send, z_recv, d_send, d_recv, f_send, f_recv,
    p_send, p_recv, h_send, h_recv, s_send, s_recv,
):
    tokens, width = fwd_ref.shape
    hidden = wd.shape[0]
    half = n // 2
    span = half // EXP_WIN
    sec, me = lax.axis_index("section"), lax.axis_index("expert")
    core, mine = lax.rem(me, 2), me // 2
    sibling = me + 1 - 2 * core
    after, ahead = lax.rem(sec + 1, sections), lax.rem(sec + sections - 1, sections)

    joined = wgu.shape[0] == 1
    if joined:
        gate_side, up_side = (wgu.at[0, :, pl.ds(i * hidden, hidden)] for i in range(2))
    else:
        gate_side, up_side = wgu.at[0], wgu.at[1]
    loads = [
        pltpu.make_async_copy(src, dst, w_sem.at[i])
        for i, (src, dst) in enumerate((
            (froute_hbm, froute_ref), (broute_hbm, broute_ref),
            (flogit_hbm, flogit_ref), (blogit_hbm, blogit_ref),
            (fwd_hbm, fwd_ref), (bwd_hbm, bwd_ref), (saved_hbm, saved_ref), (gain_hbm, gain_ref),
            (wg_hbm, gate_side), (wu_hbm, up_side), (wd_hbm, wd),
        ))
    ]
    for load in loads:
        load.start()

    barrier = pltpu.get_barrier_semaphore()
    for d in range(1, n):
        pl.semaphore_signal(
            barrier, inc=1, device_id={"expert": lax.rem(me + d, n)}, device_id_type=MESH
        )
    for where in (after, ahead):
        pl.semaphore_signal(barrier, inc=1, device_id={"section": where}, device_id_type=MESH)

    loads[0].wait()
    loads[1].wait()
    place_out[0] = place_row(froute_ref[...])
    place_out[1] = place_row(broute_ref[...])
    pl.semaphore_wait(barrier, n + 1)

    def z_copy(which, src, dst, where):
        return pltpu.make_async_remote_copy(
            src_ref=src, dst_ref=dst, send_sem=z_send.at[which], recv_sem=z_recv.at[which],
            device_id={"section": where}, device_id_type=MESH,
        )

    places = [
        z_copy(0, place_out.at[0], place_in.at[0], ahead),
        z_copy(1, place_out.at[1], place_in.at[1], after),
    ]
    heads = [
        z_copy(2, head_out.at[0], head_in.at[0], after),
        z_copy(3, head_out.at[1], head_in.at[1], ahead),
    ]
    tails = [
        z_copy(4, tail_out.at[0], stack_hbm.at[0, pl.ds(HEAD, tokens - HEAD)], after),
        z_copy(5, tail_out.at[1], stack_hbm.at[1, pl.ds(HEAD, tokens - HEAD)], ahead),
    ]
    head_keep = [
        pltpu.make_async_copy(head_in.at[i], stack_hbm.at[i, pl.ds(0, HEAD)], o_sem.at[i])
        for i in range(2)
    ]
    for copy in places:
        copy.start()

    loads[2].wait()
    loads[3].wait()
    hit, _, f_pick, f_gate, f_back = route_tables(froute_ref[...], flogit_ref[...])
    _, b_select, b_pick, b_gate, b_back = route_tables(broute_ref[...], blogit_ref[...])

    back_ref[0] = f_back
    back_ref[1] = b_back
    back_keep = pltpu.make_async_copy(back_ref, back_hbm, o_sem.at[2])
    back_keep.start()

    def peer(d):
        return lax.rem(mine + d, half)

    def direct(kind, d):
        other = peer(d)
        return pltpu.make_async_remote_copy(
            src_ref=slab.at[kind, other // span], dst_ref=rx.at[kind, core, mine],
            send_sem=d_send.at[kind, other], recv_sem=d_recv.at[kind, mine],
            device_id={"expert": 2 * other + core}, device_id_type=MESH,
        )

    def arrival(kind, d):
        other = peer(d)
        return pltpu.make_async_remote_copy(
            src_ref=slab.at[kind, 0], dst_ref=rx.at[kind, core, other],
            send_sem=d_send.at[kind, other], recv_sem=d_recv.at[kind, other],
            device_id={"expert": 2 * other + core}, device_id_type=MESH,
        )

    def forward(kind, side, other):
        return pltpu.make_async_remote_copy(
            src_ref=rx.at[kind, side, other], dst_ref=rx.at[kind, side, other],
            send_sem=f_send.at[kind, other], recv_sem=f_recv.at[kind, other],
            device_id={"expert": sibling}, device_id_type=MESH,
        )

    def dispatch(kind):
        for d in range(1, half):
            direct(kind, d).start()
        rx[kind, core, mine] = slab[kind, mine // span]
        forward(kind, core, mine).start()

    def relay(kind):
        for d in range(1, half):
            arrival(kind, d).wait_recv()
            forward(kind, core, peer(d)).start()

    def complete(kind):
        for d in range(half):
            forward(kind, 1 - core, peer(d)).wait_recv()

    def to_slab(kind, rows, at):
        for e in range(EXP_WIN):
            slab[kind, e, :, at] = rows[e * CAP : (e + 1) * CAP].astype(BF16)

    loads[4].wait()
    loads[5].wait()
    sources = (fwd_ref, bwd_ref)
    orders = []
    for which in range(2):
        places[which].wait_recv()
        orders.append(permutation(place_in[which, 0:1], tokens))

    for which in range(2):
        def fill_head(at, carry, which=which):
            head_out[which, :, at] = dot(orders[which][:HEAD], sources[which][:, at]).astype(BF16)
            return carry

        columns(width, fill_head, chunk=WIDE)
        heads[which].start()

    loads[6].wait()
    loads[7].wait()

    def gather_saved(at, total):
        rows = dot(b_select, saved_ref[:, at])
        raw[:, at] = rows
        return total + jnp.sum(rows * rows, axis=1, keepdims=True)

    square = columns(width, gather_saved, jnp.zeros((SLOTS, 1), F32), chunk=WIDE)
    saved_inv = lax.rsqrt(square / width + EPSILON)

    def norm_saved(at, carry):
        to_slab(0, raw[:, at] * saved_inv * gain_ref[:, at].astype(F32), at)
        return carry

    columns(width, norm_saved, chunk=WIDE)
    dispatch(0)

    for which in range(2):
        def fill_tail(at, carry, which=which):
            tail_out[which, :, at] = dot(orders[which][HEAD:], sources[which][:, at]).astype(BF16)
            return carry

        columns(width, fill_tail)

    logits = flogit_ref[...]
    raised = jnp.exp(logits - jnp.max(logits, axis=1, keepdims=True))
    probs = raised / jnp.sum(raised, axis=1, keepdims=True)
    count_row = jnp.sum(hit, axis=0, keepdims=True)
    prob_row = jnp.sum(probs, axis=0, keepdims=True)
    row = iota((8, EXPERTS), 0)
    stats[me] = jnp.where(row == 0, count_row, jnp.where(row == 1, prob_row, 0.0))

    def stat(d):
        other = lax.rem(me + d, n)
        return pltpu.make_async_remote_copy(
            src_ref=stats.at[me], dst_ref=stats.at[me],
            send_sem=s_send.at[other], recv_sem=s_recv.at[me],
            device_id={"expert": other}, device_id_type=MESH,
        )

    def stat_arrival(d):
        other = lax.rem(me + d, n)
        return pltpu.make_async_remote_copy(
            src_ref=stats.at[other], dst_ref=stats.at[other],
            send_sem=s_send.at[other], recv_sem=s_recv.at[other],
            device_id={"expert": other}, device_id_type=MESH,
        )

    for d in range(1, n):
        stat(d).start()

    def arrived(kind, at):
        return rx[kind, :, :, :, at].astype(F32).reshape(n * CAP, CHUNK).astype(BF16)

    zero = jnp.zeros((n * CAP, hidden), F32)

    def gate_up(kind):
        def step(at, totals):
            rows = arrived(kind, at)
            return tuple(total + dot(rows, wgu[i, at, :]) for i, total in enumerate(totals))

        empty = jnp.zeros((n * CAP, wgu.shape[2]), F32)
        totals = columns(width, step, (empty,) * wgu.shape[0])
        return (totals[0][:, :hidden], totals[0][:, hidden:]) if joined else totals

    relay(0)

    heads[1].wait_recv()
    heads[0].wait_recv()
    for copy in tails:
        copy.start()
    for copy in head_keep:
        copy.start()


    def gather_grads(at, carry):
        to_slab(1, dot(b_pick, head_in[1, :, at]) * b_gate, at)
        return carry

    columns(width, gather_grads, chunk=WIDE)
    dispatch(1)


    def gather_fwd(at, total):
        rows = dot(f_pick, head_in[0, :, at])
        wide[:, at] = rows
        return total + jnp.sum(rows * rows, axis=1, keepdims=True)

    square = columns(width, gather_fwd, jnp.zeros((SLOTS, 1), F32), chunk=WIDE)
    fwd_inv = lax.rsqrt(square / width + EPSILON)

    def norm_fwd(at, carry):
        to_slab(2, wide[:, at] * fwd_inv * gain_ref[:, at].astype(F32), at)
        return carry

    columns(width, norm_fwd, chunk=WIDE)
    dispatch(2)

    loads[8].wait()
    loads[9].wait()
    complete(0)
    gate_b, up_b = gate_up(0)
    sigma = jax.nn.sigmoid(gate_b)
    terms[0] = up_b * sigma * (1.0 + gate_b * (1.0 - sigma))
    terms[1] = gate_b * sigma
    relay(1)
    loads[10].wait()
    complete(1)

    piece = width // PIECES

    def pair(which, p):
        return pltpu.make_async_remote_copy(
            src_ref=part.at[which, p, 1 - core], dst_ref=pair_in.at[which, p],
            send_sem=p_send.at[which, p], recv_sem=p_recv.at[which, p],
            device_id={"expert": sibling}, device_id_type=MESH,
        )

    def to_home(which, p, d):
        other = peer(d)
        return pltpu.make_async_remote_copy(
            src_ref=summed.at[which, p, other], dst_ref=home.at[which, p, mine],
            send_sem=h_send.at[which, p, other], recv_sem=h_recv.at[which, p, mine],
            device_id={"expert": 2 * other + core}, device_id_type=MESH,
        )

    def from_holder(which, p, d):
        other = peer(d)
        return pltpu.make_async_remote_copy(
            src_ref=summed.at[which, p, other], dst_ref=home.at[which, p, other],
            send_sem=h_send.at[which, p, other], recv_sem=h_recv.at[which, p, other],
            device_id={"expert": 2 * other + core}, device_id_type=MESH,
        )

    def make_piece(which, p, make):
        rows = make(pl.ds(p * piece, piece))
        part[which, p] = rows.reshape(2, half, CAP, piece).astype(BF16)
        pair(which, p).start()

    def give(which, p):
        pair(which, p).wait_recv()

        def add(at, carry):
            total = part[which, p, core, :, :, at].astype(F32)
            total = total + pair_in[which, p, :, :, at].astype(F32)
            summed[which, p, :, :, at] = total.astype(BF16)
            return carry

        columns(piece, add)
        for d in range(1, half):
            to_home(which, p, d).start()
        home[which, p, mine] = summed[which, p, mine]

    d_hidden = columns(
        width,
        lambda at, total: total
        + lax.dot_general(arrived(1, at), wd[:, at], NT, preferred_element_type=F32),
        zero,
    )
    d_parts = [(d_hidden * terms[i]).astype(BF16) for i in range(2)]
    if joined:
        d_parts = [jnp.concatenate(d_parts, axis=1)]

    def input_grad(at):
        return sum(
            lax.dot_general(d_part, wgu[i, at, :], NT, preferred_element_type=F32)
            for i, d_part in enumerate(d_parts)
        )

    make_piece(0, 0, input_grad)
    make_piece(0, 1, input_grad)
    give(0, 0)
    relay(2)
    for p in range(2, PIECES):
        make_piece(0, p, input_grad)
        give(0, p - 1)
    complete(2)
    gate_f, up_f = gate_up(2)
    hidden_rows = (gate_f * jax.nn.sigmoid(gate_f) * up_f).astype(BF16)
    give(0, PIECES - 1)

    def down(at):
        return dot(hidden_rows, wd[:, at])

    make_piece(1, 0, down)
    for p in range(1, PIECES):
        make_piece(1, p, down)
        give(1, p - 1)
    give(1, PIECES - 1)

    for d in range(1, n):
        stat_arrival(d).wait_recv()
    counts = stats[0]
    for i in range(1, n):
        counts = counts + stats[i]
    tokens_all = tokens * n
    balance_ref[...] = (
        EXPERTS * (counts[0:1] / (tokens_all * TOPK)) * (counts[1:2] / tokens_all)
    )
    balance_keep = pltpu.make_async_copy(balance_ref, balance_hbm, o_sem.at[3])
    balance_keep.start()

    def returned(which, p, at):
        rows = []
        for e in range(EXP_WIN):
            total = home[which, p, e * span, :, at].astype(F32)
            for i in range(1, span):
                total = total + home[which, p, e * span + i, :, at].astype(F32)
            rows.append(total)
        return jnp.concatenate(rows, axis=0)

    def by_piece(which, p, step, init):
        for d in range(1, half):
            from_holder(which, p, d).wait_recv()

        at = pl.ds(0, piece)
        return step(pl.ds(p * piece, piece), returned(which, p, at), init)

    def weigh(at, rows, total):
        weighted = rows * gain_ref[:, at].astype(F32)
        wide[:, at] = weighted
        return total + jnp.sum(weighted * raw[:, at], axis=1, keepdims=True)

    total = jnp.zeros((SLOTS, 1), F32)
    for p in range(PIECES):
        total = by_piece(0, p, weigh, total)
    scale = saved_inv * saved_inv * saved_inv * (total / width)

    def rows_copy(which, at, i):
        rows = pl.ds(tokens, 2 * SLOTS)
        return pltpu.make_async_copy(
            halved.at[which, :, at], stack_hbm.at[which, rows, at], o_sem.at[4 + i]
        )

    def finish_bwd(at, carry):
        rows = saved_inv * wide[:, at] - raw[:, at] * scale
        halved[1, :, at] = halves(rows)
        return carry

    columns(width, finish_bwd, chunk=WIDE)
    kept = [rows_copy(1, pl.ds(0, width), PIECES)]
    kept[0].start()

    def finish_fwd(at, rows, carry):
        halved[0, :, at] = halves(rows * f_gate)
        return carry

    for p in range(PIECES):
        by_piece(1, p, finish_fwd, 0)
        kept.append(rows_copy(0, pl.ds(p * piece, piece), p))
        kept[-1].start()

    for copy in tails:
        copy.wait_recv()
    for copy in head_keep + [back_keep, balance_keep] + kept:
        copy.wait()
    for copy in places + heads + tails:
        copy.wait_send()
    for kind in range(3):
        for d in range(half):
            forward(kind, core, peer(d)).wait_send()
        for d in range(1, half):
            direct(kind, d).wait_send()
    for which in range(2):
        for p in range(PIECES):
            pair(which, p).wait_send()
            for d in range(1, half):
                to_home(which, p, d).wait_send()
    for d in range(1, n):
        stat(d).wait_send()


def place_kernel(
    stack_hbm, back_hbm, balance_hbm, fout_hbm, bout_hbm, out_hbm,
    stack, back, balance, out, in_sem, out_sem, small_sem,
):
    _, rows, width = stack.shape
    steps = width // CHUNK
    spans = [pl.ds(i * CHUNK, CHUNK) for i in range(steps)]
    small = [
        pltpu.make_async_copy(back_hbm, back, small_sem.at[0]),
        pltpu.make_async_copy(balance_hbm, balance, small_sem.at[1]),
    ]
    loads = [
        pltpu.make_async_copy(stack_hbm.at[:, :, at], stack.at[:, :, at], in_sem.at[i])
        for i, at in enumerate(spans)
    ]
    for copy in small + loads:
        copy.start()
    small[1].wait()
    last = pltpu.make_async_copy(balance, out_hbm, small_sem.at[2])
    last.start()
    small[0].wait()
    stores = []
    for i, at in enumerate(spans):
        loads[i].wait()
        for which, target in enumerate((fout_hbm, bout_hbm)):
            out[which, :, at] = dot(back[which, :, :rows], stack[which, :, at]).astype(BF16)
            store = pltpu.make_async_copy(
                out.at[which, :, at], target.at[:, at], out_sem.at[which, i]
            )
            store.start()
            stores.append(store)
    for copy in stores + [last]:
        copy.wait()


def body(
    sections, n,
    fwd_sent, bwd_sent, bwd_saved, fwd_routes, bwd_routes, fwd_logits, bwd_logits,
    norm_gain, w_gate, w_up, w_down,
):
    tokens, width = fwd_sent.shape[1:]
    hidden = w_gate.shape[2]
    half = n // 2
    hbm = pl.BlockSpec(memory_space=pl.ANY)
    dma = pltpu.SemaphoreType.DMA
    rows = tokens + 2 * SLOTS
    stack, back, balance = pl.pallas_call(
        functools.partial(kernel, sections, n),
        out_shape=(
            jax.ShapeDtypeStruct((2, rows, width), BF16),
            jax.ShapeDtypeStruct((2, tokens, EXPERTS), BF16),
            jax.ShapeDtypeStruct((1, EXPERTS), F32),
        ),
        in_specs=[hbm] * 11,
        out_specs=(hbm, hbm, hbm),
        scratch_shapes=[
            pltpu.VMEM((TOPK, tokens), jnp.int32),
            pltpu.VMEM((TOPK, tokens), jnp.int32),
            pltpu.VMEM((tokens, EXPERTS), F32),
            pltpu.VMEM((tokens, EXPERTS), F32),
            pltpu.VMEM((tokens, width), BF16),
            pltpu.VMEM((tokens, width), BF16),
            pltpu.VMEM((tokens, width), BF16),
            pltpu.VMEM((1, width), BF16),
            pltpu.VMEM((1, width, 2 * hidden) if hidden % 128 == 0 else (2, width, hidden), BF16),
            pltpu.VMEM((hidden, width), BF16),
            pltpu.VMEM((2, 8, tokens), F32),
            pltpu.VMEM((2, 8, tokens), F32),
            pltpu.VMEM((2, HEAD, width), BF16),
            pltpu.VMEM((2, tokens - HEAD, width), BF16),
            pltpu.VMEM((2, HEAD, width), BF16),
            pltpu.VMEM((2, 2 * SLOTS, width), BF16),
            pltpu.VMEM((2, tokens, EXPERTS), BF16),
            pltpu.VMEM((1, EXPERTS), F32),
            pltpu.VMEM((3, EXP_WIN, CAP, width), BF16),
            pltpu.VMEM((3, 2, half, CAP, width), BF16),
            pltpu.VMEM((2, PIECES, 2, half, CAP, width // PIECES), BF16),
            pltpu.VMEM((2, PIECES, half, CAP, width // PIECES), BF16),
            pltpu.VMEM((2, PIECES, half, CAP, width // PIECES), BF16),
            pltpu.VMEM((2, PIECES, half, CAP, width // PIECES), BF16),
            pltpu.VMEM((SLOTS, width), F32),
            pltpu.VMEM((SLOTS, width), F32),
            pltpu.VMEM((2, n * CAP, hidden), F32),
            pltpu.VMEM((n, 8, EXPERTS), F32),
            dma((11,)), dma((5 + PIECES,)), dma((6,)), dma((6,)),
            dma((3, half)), dma((3, half)), dma((3, half)), dma((3, half)),
            dma((2, PIECES)), dma((2, PIECES)), dma((2, PIECES, half)), dma((2, PIECES, half)),
            dma((n,)), dma((n,)),
        ],
        compiler_params=pltpu.CompilerParams(
            collective_id=0, has_side_effects=True, vmem_limit_bytes=60 * 1024 * 1024
        ),
    )(
        fwd_routes[0].T, bwd_routes[0].T, fwd_logits[0], bwd_logits[0],
        fwd_sent[0], bwd_sent[0], bwd_saved[0], norm_gain, w_gate[0], w_up[0], w_down[0],
    )
    fwd_out, bwd_out, balance = pl.pallas_call(
        place_kernel,
        out_shape=(
            jax.ShapeDtypeStruct((tokens, width), BF16),
            jax.ShapeDtypeStruct((tokens, width), BF16),
            jax.ShapeDtypeStruct((1, EXPERTS), F32),
        ),
        in_specs=[hbm] * 3,
        out_specs=(hbm, hbm, hbm),
        scratch_shapes=[
            pltpu.VMEM((2, rows, width), BF16),
            pltpu.VMEM((2, tokens, EXPERTS), BF16),
            pltpu.VMEM((1, EXPERTS), F32),
            pltpu.VMEM((2, tokens, width), BF16),
            dma((width // CHUNK,)), dma((2, width // CHUNK)), dma((3,)),
        ],
        compiler_params=pltpu.CompilerParams(vmem_limit_bytes=60 * 1024 * 1024),
    )(stack, back, balance)
    return fwd_out[None], bwd_out[None], balance


def solution(mesh):
    block = P("section", "expert", None)
    return jax.shard_map(
        functools.partial(body, mesh.shape["section"], mesh.shape["expert"]),
        mesh=mesh,
        in_specs=(block,) * 7
        + (
            P("section", None),
            P("section", None, "expert"),
            P("section", None, "expert"),
            P("section", "expert", None),
        ),
        out_specs=(block, block, P("section", None)),
        check_vma=False,
    )
```

```python
import functools

import jax
import jax.numpy as jnp
from jax import lax
from jax.experimental import pallas as pl
from jax.experimental.pallas import tpu as pltpu
from jax.sharding import PartitionSpec as P

EXPERTS = 128
TOPK = 8
EXP_WIN = 2
CAP = 8
SLOTS = EXP_WIN * CAP
HEAD = 16
CHUNK = 1024
WIDE = 2048
RAW = 1024
REST = 1536
PIECES = 4
EPSILON = 1e-06
MESH = pl.DeviceIdType.MESH
F32 = jnp.float32
BF16 = jnp.bfloat16
NT = (((1,), (1,)), ((), ()))


def iota(shape, dim):
    return lax.broadcasted_iota(jnp.int32, shape, dim)


def dot(a, b):
    return jnp.dot(a, b, preferred_element_type=F32)


def columns(width, body, init=0, chunk=1024):
    if chunk >= width:
        return body(pl.ds(0, width), init)

    def step(i, carry):
        return body(pl.ds(pl.multiple_of(i * chunk, chunk), chunk), carry)

    return lax.fori_loop(0, width // chunk, step, init)


def after_raw(width, body, init=0, chunk=CHUNK):
    def step(i, carry):
        return body(
            pl.ds(pl.multiple_of(i * chunk, chunk), chunk),
            pl.ds(pl.multiple_of(RAW + i * chunk, 512), chunk),
            carry,
        )

    return lax.fori_loop(0, (width - RAW) // chunk, step, init)


def route_tables(routes, logits):
    tokens, experts = logits.shape
    lane = iota((tokens, experts), 1)
    unit = (iota((tokens, tokens), 0) == iota((tokens, tokens), 1)).astype(BF16)
    routes = lax.dot_general(
        unit, routes.astype(F32).astype(BF16), NT, preferred_element_type=F32
    )
    chosen = routes[:, 0:1] == lane.astype(F32)
    for k in range(1, TOPK):
        chosen = chosen | (routes[:, k : k + 1] == lane.astype(F32))
    hit = chosen.astype(F32)
    top = jnp.max(jnp.where(chosen, logits, -jnp.inf), axis=1, keepdims=True)
    raised = jnp.exp(jnp.where(chosen, logits, top) - top) * hit
    gates = raised / jnp.sum(raised, axis=1, keepdims=True)
    here = jnp.max(jnp.where(lane < EXP_WIN, hit, 0.0), axis=1, keepdims=True)
    marks = jnp.where(lane < EXP_WIN, hit, jnp.where(lane == EXP_WIN, here, 0.0))
    below = (iota((tokens, tokens), 1) < iota((tokens, tokens), 0)).astype(BF16)
    earlier = dot(below, marks.astype(BF16))
    before = earlier[:, EXP_WIN : EXP_WIN + 1]
    count = jnp.sum(here, axis=0, keepdims=True)
    place = jnp.where(
        here > 0.0, before, count + iota((tokens, 1), 0).astype(F32) - before
    )

    def slot_at(slot):
        taken = jnp.zeros(slot.shape, F32)
        gated = jnp.zeros(slot.shape, F32)
        for e in range(EXP_WIN):
            there = (slot // CAP == e) & (
                earlier[:, e : e + 1] == (slot - e * CAP).astype(F32)
            )
            mine = jnp.where(there, hit[:, e : e + 1], 0.0)
            taken = taken + mine
            gated = gated + mine * gates[:, e : e + 1]
        return taken, gated

    taken, gated = slot_at(lane)
    taken = jnp.where(lane < SLOTS, taken, 0.0)
    gated = jnp.where(lane < SLOTS, gated, 0.0)
    turned = jnp.concatenate([taken, gated], axis=0).T
    select = turned[:SLOTS, :tokens].astype(BF16)
    right = iota((SLOTS, 2 * tokens), 1) >= tokens
    gate_slot = jnp.sum(jnp.where(right, turned[:SLOTS], 0.0), axis=1, keepdims=True)
    again = lane - tokens
    again = jnp.where(again >= SLOTS, again - SLOTS, again)
    slots_back = jnp.where(lane < tokens + 2 * SLOTS, slot_at(again)[0], 0.0)
    back, plain = (
        jnp.where(lane < tokens, (at == lane).astype(F32), slots_back).astype(BF16)
        for at in (place.astype(jnp.int32), iota((tokens, experts), 0))
    )
    head_select = dot(select, back[:, :HEAD]).astype(BF16)
    return hit, select, head_select, gate_slot, back, plain


def place_row(routes):
    tokens = routes.shape[1]
    here = jnp.max(jnp.where(routes < EXP_WIN, 1.0, 0.0), axis=0, keepdims=True)
    here = jnp.broadcast_to(here, (8, tokens))
    above = (iota((tokens, tokens), 0) < iota((tokens, tokens), 1)).astype(BF16)
    before = dot(here.astype(BF16), above)
    count = jnp.sum(here, axis=1, keepdims=True)
    order = iota((8, tokens), 1).astype(F32)
    return jnp.where(here > 0.0, before, count + order - before)


def permutation(place, tokens):
    return (iota((tokens, tokens), 0).astype(F32) == place).astype(BF16)


def halves(rows):
    high = rows.astype(BF16)
    low = (rows - high.astype(F32)).astype(BF16)
    return jnp.concatenate([high, low], axis=0)


def kernel(
    sections, n,
    froute_hbm, broute_hbm, flogit_hbm, blogit_hbm, fwd_hbm, bwd_hbm, saved_hbm, gain_hbm,
    wg_hbm, wu_hbm, wd_hbm,
    stack_hbm, back_hbm, balance_hbm,
    froute_ref, broute_ref, flogit_ref, blogit_ref, fwd_ref, bwd_ref, saved_ref, gain_ref,
    wgu, wd, place_out, place_in, head_out, tail_out, head_in,
    raw_in, halved, back_ref, balance_ref,
    slab, rx, part, pair_in, summed, home, raw, wide, terms, stats,
    w_sem, o_sem, z_send, z_recv, d_send, d_recv, f_send, f_recv,
    p_send, p_recv, h_send, h_recv, s_send, s_recv,
):
    tokens, width = fwd_ref.shape
    hidden = wd.shape[0]
    half = n // 2
    span = half // EXP_WIN
    sec, me = lax.axis_index("section"), lax.axis_index("expert")
    core, mine = lax.rem(me, 2), me // 2
    sibling = me + 1 - 2 * core
    after, ahead = lax.rem(sec + 1, sections), lax.rem(sec + sections - 1, sections)

    joined = wgu.shape[0] == 1
    if joined:
        gate_side, up_side = (wgu.at[0, :, pl.ds(i * hidden, hidden)] for i in range(2))
    else:
        gate_side, up_side = wgu.at[0], wgu.at[1]
    loads = [
        pltpu.make_async_copy(src, dst, w_sem.at[i])
        for i, (src, dst) in enumerate((
            (froute_hbm, froute_ref), (broute_hbm, broute_ref),
            (flogit_hbm, flogit_ref), (blogit_hbm, blogit_ref),
            (fwd_hbm, fwd_ref), (bwd_hbm, bwd_ref), (saved_hbm, saved_ref), (gain_hbm, gain_ref),
            (wg_hbm, gate_side), (wu_hbm, up_side), (wd_hbm, wd),
        ))
    ]
    for load in loads[:8]:
        load.start()

    barrier = pltpu.get_barrier_semaphore()
    for d in range(1, n):
        pl.semaphore_signal(
            barrier, inc=1, device_id={"expert": lax.rem(me + d, n)}, device_id_type=MESH
        )
    for where in (after, ahead):
        pl.semaphore_signal(barrier, inc=1, device_id={"section": where}, device_id_type=MESH)

    loads[0].wait()
    loads[1].wait()
    place_out[0] = place_row(froute_ref[...])
    place_out[1] = place_row(broute_ref[...])
    pl.semaphore_wait(barrier, n + 1)

    def z_copy(which, src, dst, where):
        return pltpu.make_async_remote_copy(
            src_ref=src, dst_ref=dst, send_sem=z_send.at[which], recv_sem=z_recv.at[which],
            device_id={"section": where}, device_id_type=MESH,
        )

    past = pl.ds(RAW, width - RAW)

    def tail_place(which):
        return stack_hbm.at[which, pl.ds(HEAD, tokens - HEAD), past]

    places = [
        z_copy(0, place_out.at[0], place_in.at[0], ahead),
        z_copy(1, place_out.at[1], place_in.at[1], after),
    ]
    heads = [
        z_copy(2, head_out.at[0], head_in.at[0], after),
        z_copy(3, head_out.at[1], head_in.at[1], ahead),
    ]
    tails = [
        z_copy(4, tail_out.at[0], tail_place(0), after),
        z_copy(5, tail_out.at[1], tail_place(1), ahead),
    ]
    raws = [
        z_copy(6, fwd_ref.at[:, pl.ds(0, RAW)], raw_in.at[0], after),
        z_copy(7, bwd_ref.at[:, pl.ds(0, RAW)], raw_in.at[1], ahead),
    ]
    head_keep = [
        pltpu.make_async_copy(head_in.at[i], stack_hbm.at[i, pl.ds(0, HEAD), past], o_sem.at[i])
        for i in range(2)
    ] + [
        pltpu.make_async_copy(
            raw_in.at[i], stack_hbm.at[i, pl.ds(0, tokens), pl.ds(0, RAW)],
            o_sem.at[5 + PIECES + i],
        )
        for i in range(2)
    ]
    for copy in places:
        copy.start()
    for which in range(2):
        loads[4 + which].wait()
        raws[which].start()
    for load in loads[8:]:
        load.start()

    def peer(d):
        return lax.rem(mine + d, half)

    def direct(kind, d):
        other = peer(d)
        return pltpu.make_async_remote_copy(
            src_ref=slab.at[kind, other // span], dst_ref=rx.at[kind, core, mine],
            send_sem=d_send.at[kind, other], recv_sem=d_recv.at[kind, mine],
            device_id={"expert": 2 * other + core}, device_id_type=MESH,
        )

    def arrival(kind, d):
        other = peer(d)
        return pltpu.make_async_remote_copy(
            src_ref=slab.at[kind, 0], dst_ref=rx.at[kind, core, other],
            send_sem=d_send.at[kind, other], recv_sem=d_recv.at[kind, other],
            device_id={"expert": 2 * other + core}, device_id_type=MESH,
        )

    def forward(kind, side, other):
        return pltpu.make_async_remote_copy(
            src_ref=rx.at[kind, side, other], dst_ref=rx.at[kind, side, other],
            send_sem=f_send.at[kind, other], recv_sem=f_recv.at[kind, other],
            device_id={"expert": sibling}, device_id_type=MESH,
        )

    def dispatch(kind):
        for d in range(1, half):
            direct(kind, d).start()
        rx[kind, core, mine] = slab[kind, mine // span]
        forward(kind, core, mine).start()

    def relay(kind):
        for d in range(1, half):
            arrival(kind, d).wait_recv()
            forward(kind, core, peer(d)).start()

    def complete(kind):
        for d in range(half):
            forward(kind, 1 - core, peer(d)).wait_recv()

    def to_slab(kind, rows, at):
        for e in range(EXP_WIN):
            slab[kind, e, :, at] = rows[e * CAP : (e + 1) * CAP].astype(BF16)

    loads[3].wait()
    _, b_select, b_pick, b_gate, b_back, b_plain = route_tables(broute_ref[...], blogit_ref[...])
    sources = (fwd_ref, bwd_ref)
    orders = []
    for which in range(2):
        places[which].wait_recv()
        orders.append(permutation(place_in[which, 0:1], tokens))

    for which in range(2):
        def fill_head(at, full, carry, which=which):
            rows = dot(orders[which][:HEAD], sources[which][:, full])
            head_out[which, :, at] = rows.astype(BF16)
            return carry

        after_raw(width, fill_head, chunk=REST)
        heads[which].start()

    loads[2].wait()
    hit, f_select, f_pick, f_gate, f_back, f_plain = route_tables(
        froute_ref[...], flogit_ref[...]
    )
    for i, table in enumerate((f_back, f_plain, b_back, b_plain)):
        back_ref[i] = table
    back_keep = pltpu.make_async_copy(back_ref, back_hbm, o_sem.at[2])
    back_keep.start()

    loads[6].wait()
    loads[7].wait()

    def gather_saved(at, total):
        rows = dot(b_select, saved_ref[:, at])
        raw[:, at] = rows
        return total + jnp.sum(rows * rows, axis=1, keepdims=True)

    square = columns(width, gather_saved, jnp.zeros((SLOTS, 1), F32), chunk=WIDE)
    saved_inv = lax.rsqrt(square / width + EPSILON)

    def norm_saved(at, carry):
        to_slab(0, raw[:, at] * saved_inv * gain_ref[:, at].astype(F32), at)
        return carry

    columns(width, norm_saved, chunk=WIDE)
    dispatch(0)

    for which in range(2):
        def fill_tail(at, full, carry, which=which):
            rows = dot(orders[which][HEAD:], sources[which][:, full])
            tail_out[which, :, at] = rows.astype(BF16)
            return carry

        after_raw(width, fill_tail)

    logits = flogit_ref[...]
    raised = jnp.exp(logits - jnp.max(logits, axis=1, keepdims=True))
    probs = raised / jnp.sum(raised, axis=1, keepdims=True)
    count_row = jnp.sum(hit, axis=0, keepdims=True)
    prob_row = jnp.sum(probs, axis=0, keepdims=True)
    row = iota((8, EXPERTS), 0)
    stats[me] = jnp.where(row == 0, count_row, jnp.where(row == 1, prob_row, 0.0))

    def stat(d):
        other = lax.rem(me + d, n)
        return pltpu.make_async_remote_copy(
            src_ref=stats.at[me], dst_ref=stats.at[me],
            send_sem=s_send.at[other], recv_sem=s_recv.at[me],
            device_id={"expert": other}, device_id_type=MESH,
        )

    def stat_arrival(d):
        other = lax.rem(me + d, n)
        return pltpu.make_async_remote_copy(
            src_ref=stats.at[other], dst_ref=stats.at[other],
            send_sem=s_send.at[other], recv_sem=s_recv.at[other],
            device_id={"expert": other}, device_id_type=MESH,
        )

    for d in range(1, n):
        stat(d).start()

    def arrived(kind, at):
        return rx[kind, :, :, :, at].astype(F32).reshape(n * CAP, CHUNK).astype(BF16)

    zero = jnp.zeros((n * CAP, hidden), F32)

    def gate_up(kind):
        def step(at, totals):
            rows = arrived(kind, at)
            return tuple(total + dot(rows, wgu[i, at, :]) for i, total in enumerate(totals))

        empty = jnp.zeros((n * CAP, wgu.shape[2]), F32)
        totals = columns(width, step, (empty,) * wgu.shape[0])
        return (totals[0][:, :hidden], totals[0][:, hidden:]) if joined else totals

    relay(0)

    for which in range(2):
        heads[which].wait_send()
        tails[which].start()
    for copy in raws + heads:
        copy.wait_recv()
    for copy in head_keep:
        copy.start()


    def gather_grads(at, full, carry):
        to_slab(1, dot(b_pick, head_in[1, :, at]) * b_gate, full)
        return carry

    to_slab(1, dot(b_select, raw_in[1]) * b_gate, pl.ds(0, RAW))
    after_raw(width, gather_grads, chunk=REST)
    dispatch(1)


    def gather_fwd(at, full, total):
        rows = dot(f_pick, head_in[0, :, at])
        wide[:, full] = rows
        return total + jnp.sum(rows * rows, axis=1, keepdims=True)

    first = dot(f_select, raw_in[0])
    wide[:, pl.ds(0, RAW)] = first
    square = jnp.sum(first * first, axis=1, keepdims=True)
    square = after_raw(width, gather_fwd, square, chunk=REST)
    fwd_inv = lax.rsqrt(square / width + EPSILON)

    def norm_fwd(at, carry):
        to_slab(2, wide[:, at] * fwd_inv * gain_ref[:, at].astype(F32), at)
        return carry

    columns(width, norm_fwd, chunk=WIDE)
    dispatch(2)

    loads[8].wait()
    loads[9].wait()
    complete(0)
    gate_b, up_b = gate_up(0)
    sigma = jax.nn.sigmoid(gate_b)
    terms[0] = up_b * sigma * (1.0 + gate_b * (1.0 - sigma))
    terms[1] = gate_b * sigma
    relay(1)
    loads[10].wait()
    complete(1)

    piece = width // PIECES

    def pair(which, p):
        return pltpu.make_async_remote_copy(
            src_ref=part.at[which, p, 1 - core], dst_ref=pair_in.at[which, p],
            send_sem=p_send.at[which, p], recv_sem=p_recv.at[which, p],
            device_id={"expert": sibling}, device_id_type=MESH,
        )

    def to_home(which, p, d):
        other = peer(d)
        return pltpu.make_async_remote_copy(
            src_ref=summed.at[which, p, other], dst_ref=home.at[which, p, mine],
            send_sem=h_send.at[which, p, other], recv_sem=h_recv.at[which, p, mine],
            device_id={"expert": 2 * other + core}, device_id_type=MESH,
        )

    def from_holder(which, p, d):
        other = peer(d)
        return pltpu.make_async_remote_copy(
            src_ref=summed.at[which, p, other], dst_ref=home.at[which, p, other],
            send_sem=h_send.at[which, p, other], recv_sem=h_recv.at[which, p, other],
            device_id={"expert": 2 * other + core}, device_id_type=MESH,
        )

    def make_piece(which, p, make):
        rows = make(pl.ds(p * piece, piece))
        part[which, p] = rows.reshape(2, half, CAP, piece).astype(BF16)
        pair(which, p).start()

    def give(which, p):
        pair(which, p).wait_recv()

        def add(at, carry):
            total = part[which, p, core, :, :, at].astype(F32)
            total = total + pair_in[which, p, :, :, at].astype(F32)
            summed[which, p, :, :, at] = total.astype(BF16)
            return carry

        columns(piece, add)
        for d in range(1, half):
            to_home(which, p, d).start()
        home[which, p, mine] = summed[which, p, mine]

    d_hidden = columns(
        width,
        lambda at, total: total
        + lax.dot_general(arrived(1, at), wd[:, at], NT, preferred_element_type=F32),
        zero,
    )
    d_parts = [(d_hidden * terms[i]).astype(BF16) for i in range(2)]
    if joined:
        d_parts = [jnp.concatenate(d_parts, axis=1)]

    def input_grad(at):
        return sum(
            lax.dot_general(d_part, wgu[i, at, :], NT, preferred_element_type=F32)
            for i, d_part in enumerate(d_parts)
        )

    make_piece(0, 0, input_grad)
    make_piece(0, 1, input_grad)
    give(0, 0)
    relay(2)
    for p in range(2, PIECES):
        make_piece(0, p, input_grad)
        give(0, p - 1)
    complete(2)
    gate_f, up_f = gate_up(2)
    hidden_rows = (gate_f * jax.nn.sigmoid(gate_f) * up_f).astype(BF16)
    give(0, PIECES - 1)

    def down(at):
        return dot(hidden_rows, wd[:, at])

    make_piece(1, 0, down)
    for p in range(1, PIECES):
        make_piece(1, p, down)
        give(1, p - 1)
    give(1, PIECES - 1)

    for d in range(1, n):
        stat_arrival(d).wait_recv()
    counts = stats[0]
    for i in range(1, n):
        counts = counts + stats[i]
    tokens_all = tokens * n
    balance_ref[...] = (
        EXPERTS * (counts[0:1] / (tokens_all * TOPK)) * (counts[1:2] / tokens_all)
    )
    balance_keep = pltpu.make_async_copy(balance_ref, balance_hbm, o_sem.at[3])
    balance_keep.start()

    def returned(which, p, at):
        rows = []
        for e in range(EXP_WIN):
            total = home[which, p, e * span, :, at].astype(F32)
            for i in range(1, span):
                total = total + home[which, p, e * span + i, :, at].astype(F32)
            rows.append(total)
        return jnp.concatenate(rows, axis=0)

    def by_piece(which, p, step, init):
        for d in range(1, half):
            from_holder(which, p, d).wait_recv()

        at = pl.ds(0, piece)
        return step(pl.ds(p * piece, piece), returned(which, p, at), init)

    def weigh(at, rows, total):
        weighted = rows * gain_ref[:, at].astype(F32)
        wide[:, at] = weighted
        return total + jnp.sum(weighted * raw[:, at], axis=1, keepdims=True)

    total = jnp.zeros((SLOTS, 1), F32)
    for p in range(PIECES):
        total = by_piece(0, p, weigh, total)
    scale = saved_inv * saved_inv * saved_inv * (total / width)

    def rows_copy(which, at, i):
        rows = pl.ds(tokens, 2 * SLOTS)
        return pltpu.make_async_copy(
            halved.at[which, :, at], stack_hbm.at[which, rows, at], o_sem.at[4 + i]
        )

    def finish_bwd(at, carry):
        rows = saved_inv * wide[:, at] - raw[:, at] * scale
        halved[1, :, at] = halves(rows)
        return carry

    columns(width, finish_bwd, chunk=WIDE)
    kept = [rows_copy(1, pl.ds(0, width), PIECES)]
    kept[0].start()

    def finish_fwd(at, rows, carry):
        halved[0, :, at] = halves(rows * f_gate)
        return carry

    for p in range(PIECES):
        by_piece(1, p, finish_fwd, 0)
        kept.append(rows_copy(0, pl.ds(p * piece, piece), p))
        kept[-1].start()

    for copy in tails:
        copy.wait_recv()
    for copy in head_keep + [back_keep, balance_keep] + kept:
        copy.wait()
    for copy in places + raws + tails:
        copy.wait_send()
    for kind in range(3):
        for d in range(half):
            forward(kind, core, peer(d)).wait_send()
        for d in range(1, half):
            direct(kind, d).wait_send()
    for which in range(2):
        for p in range(PIECES):
            pair(which, p).wait_send()
            for d in range(1, half):
                to_home(which, p, d).wait_send()
    for d in range(1, n):
        stat(d).wait_send()


def place_kernel(
    stack_hbm, back_hbm, balance_hbm, fout_hbm, bout_hbm, out_hbm,
    stack, back, balance, out, in_sem, out_sem, small_sem,
):
    _, rows, width = stack.shape
    steps = width // RAW
    spans = [pl.ds(i * RAW, RAW) for i in range(steps)]
    small = [
        pltpu.make_async_copy(back_hbm, back, small_sem.at[0]),
        pltpu.make_async_copy(balance_hbm, balance, small_sem.at[1]),
    ]
    loads = [
        pltpu.make_async_copy(stack_hbm.at[:, :, at], stack.at[:, :, at], in_sem.at[i])
        for i, at in enumerate(spans)
    ]
    for copy in small + loads:
        copy.start()
    small[1].wait()
    last = pltpu.make_async_copy(balance, out_hbm, small_sem.at[2])
    last.start()
    small[0].wait()
    stores = []
    for i, at in enumerate(spans):
        loads[i].wait()
        for which, target in enumerate((fout_hbm, bout_hbm)):
            table = back[2 * which + (1 if i == 0 else 0), :, :rows]
            out[which, :, at] = dot(table, stack[which, :, at]).astype(BF16)
            store = pltpu.make_async_copy(
                out.at[which, :, at], target.at[:, at], out_sem.at[which, i]
            )
            store.start()
            stores.append(store)
    for copy in stores + [last]:
        copy.wait()


def body(
    sections, n,
    fwd_sent, bwd_sent, bwd_saved, fwd_routes, bwd_routes, fwd_logits, bwd_logits,
    norm_gain, w_gate, w_up, w_down,
):
    tokens, width = fwd_sent.shape[1:]
    hidden = w_gate.shape[2]
    half = n // 2
    hbm = pl.BlockSpec(memory_space=pl.ANY)
    dma = pltpu.SemaphoreType.DMA
    rows = tokens + 2 * SLOTS
    stack, back, balance = pl.pallas_call(
        functools.partial(kernel, sections, n),
        out_shape=(
            jax.ShapeDtypeStruct((2, rows, width), BF16),
            jax.ShapeDtypeStruct((4, tokens, EXPERTS), BF16),
            jax.ShapeDtypeStruct((1, EXPERTS), F32),
        ),
        in_specs=[hbm] * 11,
        out_specs=(hbm, hbm, hbm),
        scratch_shapes=[
            pltpu.VMEM((TOPK, tokens), jnp.int32),
            pltpu.VMEM((TOPK, tokens), jnp.int32),
            pltpu.VMEM((tokens, EXPERTS), F32),
            pltpu.VMEM((tokens, EXPERTS), F32),
            pltpu.VMEM((tokens, width), BF16),
            pltpu.VMEM((tokens, width), BF16),
            pltpu.VMEM((tokens, width), BF16),
            pltpu.VMEM((1, width), BF16),
            pltpu.VMEM((1, width, 2 * hidden) if hidden % 128 == 0 else (2, width, hidden), BF16),
            pltpu.VMEM((hidden, width), BF16),
            pltpu.VMEM((2, 8, tokens), F32),
            pltpu.VMEM((2, 8, tokens), F32),
            pltpu.VMEM((2, HEAD, width - RAW), BF16),
            pltpu.VMEM((2, tokens - HEAD, width - RAW), BF16),
            pltpu.VMEM((2, HEAD, width - RAW), BF16),
            pltpu.VMEM((2, tokens, RAW), BF16),
            pltpu.VMEM((2, 2 * SLOTS, width), BF16),
            pltpu.VMEM((4, tokens, EXPERTS), BF16),
            pltpu.VMEM((1, EXPERTS), F32),
            pltpu.VMEM((3, EXP_WIN, CAP, width), BF16),
            pltpu.VMEM((3, 2, half, CAP, width), BF16),
            pltpu.VMEM((2, PIECES, 2, half, CAP, width // PIECES), BF16),
            pltpu.VMEM((2, PIECES, half, CAP, width // PIECES), BF16),
            pltpu.VMEM((2, PIECES, half, CAP, width // PIECES), BF16),
            pltpu.VMEM((2, PIECES, half, CAP, width // PIECES), BF16),
            pltpu.VMEM((SLOTS, width), F32),
            pltpu.VMEM((SLOTS, width), F32),
            pltpu.VMEM((2, n * CAP, hidden), F32),
            pltpu.VMEM((n, 8, EXPERTS), F32),
            dma((11,)), dma((7 + PIECES,)), dma((8,)), dma((8,)),
            dma((3, half)), dma((3, half)), dma((3, half)), dma((3, half)),
            dma((2, PIECES)), dma((2, PIECES)), dma((2, PIECES, half)), dma((2, PIECES, half)),
            dma((n,)), dma((n,)),
        ],
        compiler_params=pltpu.CompilerParams(
            collective_id=0, has_side_effects=True, vmem_limit_bytes=60 * 1024 * 1024
        ),
    )(
        fwd_routes[0].T, bwd_routes[0].T, fwd_logits[0], bwd_logits[0],
        fwd_sent[0], bwd_sent[0], bwd_saved[0], norm_gain, w_gate[0], w_up[0], w_down[0],
    )
    fwd_out, bwd_out, balance = pl.pallas_call(
        place_kernel,
        out_shape=(
            jax.ShapeDtypeStruct((tokens, width), BF16),
            jax.ShapeDtypeStruct((tokens, width), BF16),
            jax.ShapeDtypeStruct((1, EXPERTS), F32),
        ),
        in_specs=[hbm] * 3,
        out_specs=(hbm, hbm, hbm),
        scratch_shapes=[
            pltpu.VMEM((2, rows, width), BF16),
            pltpu.VMEM((4, tokens, EXPERTS), BF16),
            pltpu.VMEM((1, EXPERTS), F32),
            pltpu.VMEM((2, tokens, width), BF16),
            dma((width // RAW,)), dma((2, width // RAW)), dma((3,)),
        ],
        compiler_params=pltpu.CompilerParams(vmem_limit_bytes=60 * 1024 * 1024),
    )(stack, back, balance)
    return fwd_out[None], bwd_out[None], balance


def solution(mesh):
    block = P("section", "expert", None)
    return jax.shard_map(
        functools.partial(body, mesh.shape["section"], mesh.shape["expert"]),
        mesh=mesh,
        in_specs=(block,) * 7
        + (
            P("section", None),
            P("section", None, "expert"),
            P("section", None, "expert"),
            P("section", "expert", None),
        ),
        out_specs=(block, block, P("section", None)),
        check_vma=False,
    )
```

```python
import functools

import jax
import jax.numpy as jnp
from jax import lax
from jax.experimental import pallas as pl
from jax.experimental.pallas import tpu as pltpu
from jax.sharding import PartitionSpec as P

EXPERTS = 128
TOPK = 8
EXP_WIN = 2
CAP = 8
SLOTS = EXP_WIN * CAP
HEAD = 16
CHUNK = 1024
WIDE = 2048
PIECES = 4
EPSILON = 1e-06
MESH = pl.DeviceIdType.MESH
F32 = jnp.float32
BF16 = jnp.bfloat16
NT = (((1,), (1,)), ((), ()))


def iota(shape, dim):
    return lax.broadcasted_iota(jnp.int32, shape, dim)


def dot(a, b):
    return jnp.dot(a, b, preferred_element_type=F32)


def columns(width, body, init=0, chunk=1024):
    if chunk >= width:
        return body(pl.ds(0, width), init)

    def step(i, carry):
        return body(pl.ds(pl.multiple_of(i * chunk, chunk), chunk), carry)

    return lax.fori_loop(0, width // chunk, step, init)


def route_tables(routes, logits):
    tokens, experts = logits.shape
    lane = iota((tokens, experts), 1)
    unit = (iota((tokens, tokens), 0) == iota((tokens, tokens), 1)).astype(BF16)
    routes = lax.dot_general(
        unit, routes.astype(F32).astype(BF16), NT, preferred_element_type=F32
    )
    chosen = routes[:, 0:1] == lane.astype(F32)
    for k in range(1, TOPK):
        chosen = chosen | (routes[:, k : k + 1] == lane.astype(F32))
    hit = chosen.astype(F32)
    top = jnp.max(jnp.where(chosen, logits, -jnp.inf), axis=1, keepdims=True)
    raised = jnp.exp(jnp.where(chosen, logits, top) - top) * hit
    gates = raised / jnp.sum(raised, axis=1, keepdims=True)
    here = jnp.max(jnp.where(lane < EXP_WIN, hit, 0.0), axis=1, keepdims=True)
    marks = jnp.where(lane < EXP_WIN, hit, jnp.where(lane == EXP_WIN, here, 0.0))
    below = (iota((tokens, tokens), 1) < iota((tokens, tokens), 0)).astype(BF16)
    earlier = dot(below, marks.astype(BF16))
    before = earlier[:, EXP_WIN : EXP_WIN + 1]
    count = jnp.sum(here, axis=0, keepdims=True)
    place = jnp.where(
        here > 0.0, before, count + iota((tokens, 1), 0).astype(F32) - before
    )

    def slot_at(slot):
        taken = jnp.zeros(slot.shape, F32)
        gated = jnp.zeros(slot.shape, F32)
        for e in range(EXP_WIN):
            there = (slot // CAP == e) & (
                earlier[:, e : e + 1] == (slot - e * CAP).astype(F32)
            )
            mine = jnp.where(there, hit[:, e : e + 1], 0.0)
            taken = taken + mine
            gated = gated + mine * gates[:, e : e + 1]
        return taken, gated

    taken, gated = slot_at(lane)
    taken = jnp.where(lane < SLOTS, taken, 0.0)
    gated = jnp.where(lane < SLOTS, gated, 0.0)
    turned = jnp.concatenate([taken, gated], axis=0).T
    select = turned[:SLOTS, :tokens].astype(BF16)
    right = iota((SLOTS, 2 * tokens), 1) >= tokens
    gate_slot = jnp.sum(jnp.where(right, turned[:SLOTS], 0.0), axis=1, keepdims=True)
    again = lane - tokens
    again = jnp.where(again >= SLOTS, again - SLOTS, again)
    back = jnp.where(
        lane < tokens,
        (place == lane.astype(F32)).astype(F32),
        jnp.where(lane < tokens + 2 * SLOTS, slot_at(again)[0], 0.0),
    ).astype(BF16)
    head_select = dot(select, back[:, :HEAD]).astype(BF16)
    return hit, select, head_select, gate_slot, back


def place_row(routes):
    tokens = routes.shape[1]
    here = jnp.max(jnp.where(routes < EXP_WIN, 1.0, 0.0), axis=0, keepdims=True)
    here = jnp.broadcast_to(here, (8, tokens))
    above = (iota((tokens, tokens), 0) < iota((tokens, tokens), 1)).astype(BF16)
    before = dot(here.astype(BF16), above)
    count = jnp.sum(here, axis=1, keepdims=True)
    order = iota((8, tokens), 1).astype(F32)
    return jnp.where(here > 0.0, before, count + order - before)


def permutation(place, tokens):
    return (iota((tokens, tokens), 0).astype(F32) == place).astype(BF16)


def halves(rows):
    high = rows.astype(BF16)
    low = (rows - high.astype(F32)).astype(BF16)
    return jnp.concatenate([high, low], axis=0)


def kernel(
    sections, n,
    froute_hbm, broute_hbm, flogit_hbm, blogit_hbm, fwd_hbm, bwd_hbm, saved_hbm, gain_hbm,
    wg_hbm, wu_hbm, wd_hbm,
    stack_hbm, back_hbm, balance_hbm,
    froute_ref, broute_ref, flogit_ref, blogit_ref, fwd_ref, bwd_ref, saved_ref, gain_ref,
    wgu, wd, place_out, place_in, head_out, tail_out, head_in,
    halved, back_ref, balance_ref,
    slab, rx, part, pair_in, summed, home, raw, wide, terms, stats,
    w_sem, o_sem, z_send, z_recv, d_send, d_recv, f_send, f_recv,
    p_send, p_recv, h_send, h_recv, s_send, s_recv,
):
    tokens, width = fwd_ref.shape
    hidden = wd.shape[0]
    half = n // 2
    span = half // EXP_WIN
    sec, me = lax.axis_index("section"), lax.axis_index("expert")
    core, mine = lax.rem(me, 2), me // 2
    sibling = me + 1 - 2 * core
    after, ahead = lax.rem(sec + 1, sections), lax.rem(sec + sections - 1, sections)

    joined = wgu.shape[0] == 1
    if joined:
        gate_side, up_side = (wgu.at[0, :, pl.ds(i * hidden, hidden)] for i in range(2))
    else:
        gate_side, up_side = wgu.at[0], wgu.at[1]
    loads = [
        pltpu.make_async_copy(src, dst, w_sem.at[i])
        for i, (src, dst) in enumerate((
            (froute_hbm, froute_ref), (broute_hbm, broute_ref),
            (flogit_hbm, flogit_ref), (blogit_hbm, blogit_ref),
            (fwd_hbm, fwd_ref), (bwd_hbm, bwd_ref), (saved_hbm, saved_ref), (gain_hbm, gain_ref),
            (wg_hbm, gate_side), (wu_hbm, up_side), (wd_hbm, wd),
        ))
    ]
    for load in loads[:8]:
        load.start()

    barrier = pltpu.get_barrier_semaphore()
    for d in range(1, n):
        pl.semaphore_signal(
            barrier, inc=1, device_id={"expert": lax.rem(me + d, n)}, device_id_type=MESH
        )
    for where in (after, ahead):
        pl.semaphore_signal(barrier, inc=1, device_id={"section": where}, device_id_type=MESH)

    loads[0].wait()
    loads[1].wait()
    place_out[0] = place_row(froute_ref[...])
    place_out[1] = place_row(broute_ref[...])
    pl.semaphore_wait(barrier, n + 1)

    def z_copy(which, src, dst, where):
        return pltpu.make_async_remote_copy(
            src_ref=src, dst_ref=dst, send_sem=z_send.at[which], recv_sem=z_recv.at[which],
            device_id={"section": where}, device_id_type=MESH,
        )

    places = [
        z_copy(0, place_out.at[0], place_in.at[0], ahead),
        z_copy(1, place_out.at[1], place_in.at[1], after),
    ]
    heads = [
        z_copy(2, head_out.at[0], head_in.at[0], after),
        z_copy(3, head_out.at[1], head_in.at[1], ahead),
    ]
    tails = [
        z_copy(4, tail_out.at[0], stack_hbm.at[0, pl.ds(HEAD, tokens - HEAD)], after),
        z_copy(5, tail_out.at[1], stack_hbm.at[1, pl.ds(HEAD, tokens - HEAD)], ahead),
    ]
    head_keep = [
        pltpu.make_async_copy(head_in.at[i], stack_hbm.at[i, pl.ds(0, HEAD)], o_sem.at[i])
        for i in range(2)
    ]
    for copy in places:
        copy.start()
    for load in loads[8:]:
        load.start()

    def peer(d):
        return lax.rem(mine + d, half)

    def direct(kind, d):
        other = peer(d)
        return pltpu.make_async_remote_copy(
            src_ref=slab.at[kind, other // span], dst_ref=rx.at[kind, core, mine],
            send_sem=d_send.at[kind, other], recv_sem=d_recv.at[kind, mine],
            device_id={"expert": 2 * other + core}, device_id_type=MESH,
        )

    def arrival(kind, d):
        other = peer(d)
        return pltpu.make_async_remote_copy(
            src_ref=slab.at[kind, 0], dst_ref=rx.at[kind, core, other],
            send_sem=d_send.at[kind, other], recv_sem=d_recv.at[kind, other],
            device_id={"expert": 2 * other + core}, device_id_type=MESH,
        )

    def forward(kind, side, other):
        return pltpu.make_async_remote_copy(
            src_ref=rx.at[kind, side, other], dst_ref=rx.at[kind, side, other],
            send_sem=f_send.at[kind, other], recv_sem=f_recv.at[kind, other],
            device_id={"expert": sibling}, device_id_type=MESH,
        )

    def dispatch(kind):
        for d in range(1, half):
            direct(kind, d).start()
        rx[kind, core, mine] = slab[kind, mine // span]
        forward(kind, core, mine).start()

    def relay(kind):
        for d in range(1, half):
            arrival(kind, d).wait_recv()
            forward(kind, core, peer(d)).start()

    def complete(kind):
        for d in range(half):
            forward(kind, 1 - core, peer(d)).wait_recv()

    def to_slab(kind, rows, at):
        for e in range(EXP_WIN):
            slab[kind, e, :, at] = rows[e * CAP : (e + 1) * CAP].astype(BF16)

    loads[3].wait()
    _, b_select, b_pick, b_gate, b_back = route_tables(broute_ref[...], blogit_ref[...])
    loads[4].wait()
    loads[5].wait()
    sources = (fwd_ref, bwd_ref)
    orders = []
    for which in range(2):
        places[which].wait_recv()
        orders.append(permutation(place_in[which, 0:1], tokens))

    for which in (1, 0):
        def fill_head(at, carry, which=which):
            head_out[which, :, at] = dot(orders[which][:HEAD], sources[which][:, at]).astype(BF16)
            return carry

        columns(width, fill_head, chunk=WIDE)
        heads[which].start()

    loads[6].wait()
    loads[7].wait()

    def gather_saved(at, total):
        rows = dot(b_select, saved_ref[:, at])
        raw[:, at] = rows
        return total + jnp.sum(rows * rows, axis=1, keepdims=True)

    square = columns(width, gather_saved, jnp.zeros((SLOTS, 1), F32), chunk=WIDE)
    saved_inv = lax.rsqrt(square / width + EPSILON)

    def norm_saved(at, carry):
        to_slab(0, raw[:, at] * saved_inv * gain_ref[:, at].astype(F32), at)
        return carry

    columns(width, norm_saved, chunk=WIDE)
    dispatch(0)

    loads[2].wait()
    hit, _, f_pick, f_gate, f_back = route_tables(froute_ref[...], flogit_ref[...])
    back_ref[0] = f_back
    back_ref[1] = b_back
    back_keep = pltpu.make_async_copy(back_ref, back_hbm, o_sem.at[2])
    back_keep.start()

    for which in range(2):
        def fill_tail(at, carry, which=which):
            tail_out[which, :, at] = dot(orders[which][HEAD:], sources[which][:, at]).astype(BF16)
            return carry

        columns(width, fill_tail)

    logits = flogit_ref[...]
    raised = jnp.exp(logits - jnp.max(logits, axis=1, keepdims=True))
    probs = raised / jnp.sum(raised, axis=1, keepdims=True)
    count_row = jnp.sum(hit, axis=0, keepdims=True)
    prob_row = jnp.sum(probs, axis=0, keepdims=True)
    row = iota((8, EXPERTS), 0)
    stats[me] = jnp.where(row == 0, count_row, jnp.where(row == 1, prob_row, 0.0))

    def stat(d):
        other = lax.rem(me + d, n)
        return pltpu.make_async_remote_copy(
            src_ref=stats.at[me], dst_ref=stats.at[me],
            send_sem=s_send.at[other], recv_sem=s_recv.at[me],
            device_id={"expert": other}, device_id_type=MESH,
        )

    def stat_arrival(d):
        other = lax.rem(me + d, n)
        return pltpu.make_async_remote_copy(
            src_ref=stats.at[other], dst_ref=stats.at[other],
            send_sem=s_send.at[other], recv_sem=s_recv.at[other],
            device_id={"expert": other}, device_id_type=MESH,
        )

    for d in range(1, n):
        stat(d).start()

    def arrived(kind, at):
        return rx[kind, :, :, :, at].astype(F32).reshape(n * CAP, CHUNK).astype(BF16)

    zero = jnp.zeros((n * CAP, hidden), F32)

    def gate_up(kind):
        def step(at, totals):
            rows = arrived(kind, at)
            return tuple(total + dot(rows, wgu[i, at, :]) for i, total in enumerate(totals))

        empty = jnp.zeros((n * CAP, wgu.shape[2]), F32)
        totals = columns(width, step, (empty,) * wgu.shape[0])
        return (totals[0][:, :hidden], totals[0][:, hidden:]) if joined else totals

    relay(0)

    heads[1].wait_recv()
    heads[0].wait_recv()
    for copy in tails:
        copy.start()
    for copy in head_keep:
        copy.start()


    def gather_grads(at, carry):
        to_slab(1, dot(b_pick, head_in[1, :, at]) * b_gate, at)
        return carry

    columns(width, gather_grads, chunk=WIDE)
    dispatch(1)


    def gather_fwd(at, total):
        rows = dot(f_pick, head_in[0, :, at])
        wide[:, at] = rows
        return total + jnp.sum(rows * rows, axis=1, keepdims=True)

    square = columns(width, gather_fwd, jnp.zeros((SLOTS, 1), F32), chunk=WIDE)
    fwd_inv = lax.rsqrt(square / width + EPSILON)

    def norm_fwd(at, carry):
        to_slab(2, wide[:, at] * fwd_inv * gain_ref[:, at].astype(F32), at)
        return carry

    columns(width, norm_fwd, chunk=WIDE)
    dispatch(2)

    loads[8].wait()
    loads[9].wait()
    complete(0)
    gate_b, up_b = gate_up(0)
    sigma = jax.nn.sigmoid(gate_b)
    terms[0] = up_b * sigma * (1.0 + gate_b * (1.0 - sigma))
    terms[1] = gate_b * sigma
    relay(1)
    loads[10].wait()
    complete(1)

    piece = width // PIECES

    def pair(which, p):
        return pltpu.make_async_remote_copy(
            src_ref=part.at[which, p, 1 - core], dst_ref=pair_in.at[which, p],
            send_sem=p_send.at[which, p], recv_sem=p_recv.at[which, p],
            device_id={"expert": sibling}, device_id_type=MESH,
        )

    def to_home(which, p, d):
        other = peer(d)
        return pltpu.make_async_remote_copy(
            src_ref=summed.at[which, p, other], dst_ref=home.at[which, p, mine],
            send_sem=h_send.at[which, p, other], recv_sem=h_recv.at[which, p, mine],
            device_id={"expert": 2 * other + core}, device_id_type=MESH,
        )

    def from_holder(which, p, d):
        other = peer(d)
        return pltpu.make_async_remote_copy(
            src_ref=summed.at[which, p, other], dst_ref=home.at[which, p, other],
            send_sem=h_send.at[which, p, other], recv_sem=h_recv.at[which, p, other],
            device_id={"expert": 2 * other + core}, device_id_type=MESH,
        )

    def make_piece(which, p, make):
        rows = make(pl.ds(p * piece, piece))
        part[which, p] = rows.reshape(2, half, CAP, piece).astype(BF16)
        pair(which, p).start()

    def give(which, p):
        pair(which, p).wait_recv()

        def add(at, carry):
            total = part[which, p, core, :, :, at].astype(F32)
            total = total + pair_in[which, p, :, :, at].astype(F32)
            summed[which, p, :, :, at] = total.astype(BF16)
            return carry

        columns(piece, add)
        for d in range(1, half):
            to_home(which, p, d).start()
        home[which, p, mine] = summed[which, p, mine]

    d_hidden = columns(
        width,
        lambda at, total: total
        + lax.dot_general(arrived(1, at), wd[:, at], NT, preferred_element_type=F32),
        zero,
    )
    d_parts = [(d_hidden * terms[i]).astype(BF16) for i in range(2)]
    if joined:
        d_parts = [jnp.concatenate(d_parts, axis=1)]

    def input_grad(at):
        return sum(
            lax.dot_general(d_part, wgu[i, at, :], NT, preferred_element_type=F32)
            for i, d_part in enumerate(d_parts)
        )

    relay(2)
    make_piece(0, 0, input_grad)
    make_piece(0, 1, input_grad)
    give(0, 0)
    for p in range(2, PIECES):
        make_piece(0, p, input_grad)
        give(0, p - 1)
    complete(2)
    gate_f, up_f = gate_up(2)
    hidden_rows = (gate_f * jax.nn.sigmoid(gate_f) * up_f).astype(BF16)
    give(0, PIECES - 1)

    def down(at):
        return dot(hidden_rows, wd[:, at])

    make_piece(1, 0, down)
    for p in range(1, PIECES):
        make_piece(1, p, down)
        give(1, p - 1)
    give(1, PIECES - 1)

    for d in range(1, n):
        stat_arrival(d).wait_recv()
    counts = stats[0]
    for i in range(1, n):
        counts = counts + stats[i]
    tokens_all = tokens * n
    balance_ref[...] = (
        EXPERTS * (counts[0:1] / (tokens_all * TOPK)) * (counts[1:2] / tokens_all)
    )
    balance_keep = pltpu.make_async_copy(balance_ref, balance_hbm, o_sem.at[3])
    balance_keep.start()

    def returned(which, p, at):
        rows = []
        for e in range(EXP_WIN):
            total = home[which, p, e * span, :, at].astype(F32)
            for i in range(1, span):
                total = total + home[which, p, e * span + i, :, at].astype(F32)
            rows.append(total)
        return jnp.concatenate(rows, axis=0)

    def by_piece(which, p, step, init):
        for d in range(1, half):
            from_holder(which, p, d).wait_recv()

        at = pl.ds(0, piece)
        return step(pl.ds(p * piece, piece), returned(which, p, at), init)

    def weigh(at, rows, total):
        weighted = rows * gain_ref[:, at].astype(F32)
        wide[:, at] = weighted
        return total + jnp.sum(weighted * raw[:, at], axis=1, keepdims=True)

    total = jnp.zeros((SLOTS, 1), F32)
    for p in range(PIECES):
        total = by_piece(0, p, weigh, total)
    scale = saved_inv * saved_inv * saved_inv * (total / width)

    def rows_copy(which, at, i):
        rows = pl.ds(tokens, 2 * SLOTS)
        return pltpu.make_async_copy(
            halved.at[which, :, at], stack_hbm.at[which, rows, at], o_sem.at[4 + i]
        )

    def finish_bwd(at, carry):
        rows = saved_inv * wide[:, at] - raw[:, at] * scale
        halved[1, :, at] = halves(rows)
        return carry

    columns(width, finish_bwd, chunk=WIDE)
    kept = [rows_copy(1, pl.ds(0, width), PIECES)]
    kept[0].start()

    def finish_fwd(at, rows, carry):
        halved[0, :, at] = halves(rows * f_gate)
        return carry

    for p in range(PIECES):
        by_piece(1, p, finish_fwd, 0)
        kept.append(rows_copy(0, pl.ds(p * piece, piece), p))
        kept[-1].start()

    for copy in tails:
        copy.wait_recv()
    for copy in head_keep + [back_keep, balance_keep] + kept:
        copy.wait()
    for copy in places + heads + tails:
        copy.wait_send()
    for kind in range(3):
        for d in range(half):
            forward(kind, core, peer(d)).wait_send()
        for d in range(1, half):
            direct(kind, d).wait_send()
    for which in range(2):
        for p in range(PIECES):
            pair(which, p).wait_send()
            for d in range(1, half):
                to_home(which, p, d).wait_send()
    for d in range(1, n):
        stat(d).wait_send()


def place_kernel(
    stack_hbm, back_hbm, balance_hbm, fout_hbm, bout_hbm, out_hbm,
    stack, back, balance, out, in_sem, out_sem, small_sem,
):
    _, rows, width = stack.shape
    steps = width // CHUNK
    spans = [pl.ds(i * CHUNK, CHUNK) for i in range(steps)]
    small = [
        pltpu.make_async_copy(back_hbm, back, small_sem.at[0]),
        pltpu.make_async_copy(balance_hbm, balance, small_sem.at[1]),
    ]
    loads = [
        pltpu.make_async_copy(stack_hbm.at[:, :, at], stack.at[:, :, at], in_sem.at[i])
        for i, at in enumerate(spans)
    ]
    for copy in small + loads:
        copy.start()
    small[1].wait()
    last = pltpu.make_async_copy(balance, out_hbm, small_sem.at[2])
    last.start()
    small[0].wait()
    stores = []
    for i, at in enumerate(spans):
        loads[i].wait()
        for which, target in enumerate((fout_hbm, bout_hbm)):
            out[which, :, at] = dot(back[which, :, :rows], stack[which, :, at]).astype(BF16)
            store = pltpu.make_async_copy(
                out.at[which, :, at], target.at[:, at], out_sem.at[which, i]
            )
            store.start()
            stores.append(store)
    for copy in stores + [last]:
        copy.wait()


def body(
    sections, n,
    fwd_sent, bwd_sent, bwd_saved, fwd_routes, bwd_routes, fwd_logits, bwd_logits,
    norm_gain, w_gate, w_up, w_down,
):
    tokens, width = fwd_sent.shape[1:]
    hidden = w_gate.shape[2]
    half = n // 2
    hbm = pl.BlockSpec(memory_space=pl.ANY)
    dma = pltpu.SemaphoreType.DMA
    rows = tokens + 2 * SLOTS
    stack, back, balance = pl.pallas_call(
        functools.partial(kernel, sections, n),
        out_shape=(
            jax.ShapeDtypeStruct((2, rows, width), BF16),
            jax.ShapeDtypeStruct((2, tokens, EXPERTS), BF16),
            jax.ShapeDtypeStruct((1, EXPERTS), F32),
        ),
        in_specs=[hbm] * 11,
        out_specs=(hbm, hbm, hbm),
        scratch_shapes=[
            pltpu.VMEM((TOPK, tokens), jnp.int32),
            pltpu.VMEM((TOPK, tokens), jnp.int32),
            pltpu.VMEM((tokens, EXPERTS), F32),
            pltpu.VMEM((tokens, EXPERTS), F32),
            pltpu.VMEM((tokens, width), BF16),
            pltpu.VMEM((tokens, width), BF16),
            pltpu.VMEM((tokens, width), BF16),
            pltpu.VMEM((1, width), BF16),
            pltpu.VMEM((1, width, 2 * hidden) if hidden % 128 == 0 else (2, width, hidden), BF16),
            pltpu.VMEM((hidden, width), BF16),
            pltpu.VMEM((2, 8, tokens), F32),
            pltpu.VMEM((2, 8, tokens), F32),
            pltpu.VMEM((2, HEAD, width), BF16),
            pltpu.VMEM((2, tokens - HEAD, width), BF16),
            pltpu.VMEM((2, HEAD, width), BF16),
            pltpu.VMEM((2, 2 * SLOTS, width), BF16),
            pltpu.VMEM((2, tokens, EXPERTS), BF16),
            pltpu.VMEM((1, EXPERTS), F32),
            pltpu.VMEM((3, EXP_WIN, CAP, width), BF16),
            pltpu.VMEM((3, 2, half, CAP, width), BF16),
            pltpu.VMEM((2, PIECES, 2, half, CAP, width // PIECES), BF16),
            pltpu.VMEM((2, PIECES, half, CAP, width // PIECES), BF16),
            pltpu.VMEM((2, PIECES, half, CAP, width // PIECES), BF16),
            pltpu.VMEM((2, PIECES, half, CAP, width // PIECES), BF16),
            pltpu.VMEM((SLOTS, width), F32),
            pltpu.VMEM((SLOTS, width), F32),
            pltpu.VMEM((2, n * CAP, hidden), F32),
            pltpu.VMEM((n, 8, EXPERTS), F32),
            dma((11,)), dma((5 + PIECES,)), dma((6,)), dma((6,)),
            dma((3, half)), dma((3, half)), dma((3, half)), dma((3, half)),
            dma((2, PIECES)), dma((2, PIECES)), dma((2, PIECES, half)), dma((2, PIECES, half)),
            dma((n,)), dma((n,)),
        ],
        compiler_params=pltpu.CompilerParams(
            collective_id=0, has_side_effects=True, vmem_limit_bytes=60 * 1024 * 1024
        ),
    )(
        fwd_routes[0].T, bwd_routes[0].T, fwd_logits[0], bwd_logits[0],
        fwd_sent[0], bwd_sent[0], bwd_saved[0], norm_gain, w_gate[0], w_up[0], w_down[0],
    )
    fwd_out, bwd_out, balance = pl.pallas_call(
        place_kernel,
        out_shape=(
            jax.ShapeDtypeStruct((tokens, width), BF16),
            jax.ShapeDtypeStruct((tokens, width), BF16),
            jax.ShapeDtypeStruct((1, EXPERTS), F32),
        ),
        in_specs=[hbm] * 3,
        out_specs=(hbm, hbm, hbm),
        scratch_shapes=[
            pltpu.VMEM((2, rows, width), BF16),
            pltpu.VMEM((2, tokens, EXPERTS), BF16),
            pltpu.VMEM((1, EXPERTS), F32),
            pltpu.VMEM((2, tokens, width), BF16),
            dma((width // CHUNK,)), dma((2, width // CHUNK)), dma((3,)),
        ],
        compiler_params=pltpu.CompilerParams(vmem_limit_bytes=60 * 1024 * 1024),
    )(stack, back, balance)
    return fwd_out[None], bwd_out[None], balance


def solution(mesh):
    block = P("section", "expert", None)
    return jax.shard_map(
        functools.partial(body, mesh.shape["section"], mesh.shape["expert"]),
        mesh=mesh,
        in_specs=(block,) * 7
        + (
            P("section", None),
            P("section", None, "expert"),
            P("section", None, "expert"),
            P("section", "expert", None),
        ),
        out_specs=(block, block, P("section", None)),
        check_vma=False,
    )
```

```python
import functools

import jax
import jax.numpy as jnp
from jax import lax
from jax.experimental import pallas as pl
from jax.experimental.pallas import tpu as pltpu
from jax.sharding import PartitionSpec as P

EXPERTS = 128
TOPK = 8
EXP_WIN = 2
CAP = 8
SLOTS = EXP_WIN * CAP
HEAD = 16
CHUNK = 1024
WIDE = 2048
PIECES = 2
EPSILON = 1e-06
MESH = pl.DeviceIdType.MESH
F32 = jnp.float32
BF16 = jnp.bfloat16
NT = (((1,), (1,)), ((), ()))


def iota(shape, dim):
    return lax.broadcasted_iota(jnp.int32, shape, dim)


def dot(a, b):
    return jnp.dot(a, b, preferred_element_type=F32)


def columns(width, body, init=0, chunk=1024):
    if chunk >= width:
        return body(pl.ds(0, width), init)

    def step(i, carry):
        return body(pl.ds(pl.multiple_of(i * chunk, chunk), chunk), carry)

    return lax.fori_loop(0, width // chunk, step, init)


def route_tables(routes, logits):
    tokens, experts = logits.shape
    lane = iota((tokens, experts), 1)
    unit = (iota((tokens, tokens), 0) == iota((tokens, tokens), 1)).astype(BF16)
    routes = lax.dot_general(
        unit, routes.astype(F32).astype(BF16), NT, preferred_element_type=F32
    )
    chosen = routes[:, 0:1] == lane.astype(F32)
    for k in range(1, TOPK):
        chosen = chosen | (routes[:, k : k + 1] == lane.astype(F32))
    hit = chosen.astype(F32)
    top = jnp.max(jnp.where(chosen, logits, -jnp.inf), axis=1, keepdims=True)
    raised = jnp.exp(jnp.where(chosen, logits, top) - top) * hit
    gates = raised / jnp.sum(raised, axis=1, keepdims=True)
    here = jnp.max(jnp.where(lane < EXP_WIN, hit, 0.0), axis=1, keepdims=True)
    marks = jnp.where(lane < EXP_WIN, hit, jnp.where(lane == EXP_WIN, here, 0.0))
    below = (iota((tokens, tokens), 1) < iota((tokens, tokens), 0)).astype(BF16)
    earlier = dot(below, marks.astype(BF16))
    before = earlier[:, EXP_WIN : EXP_WIN + 1]
    count = jnp.sum(here, axis=0, keepdims=True)
    place = jnp.where(
        here > 0.0, before, count + iota((tokens, 1), 0).astype(F32) - before
    )

    def slot_at(slot):
        taken = jnp.zeros(slot.shape, F32)
        gated = jnp.zeros(slot.shape, F32)
        for e in range(EXP_WIN):
            there = (slot // CAP == e) & (
                earlier[:, e : e + 1] == (slot - e * CAP).astype(F32)
            )
            mine = jnp.where(there, hit[:, e : e + 1], 0.0)
            taken = taken + mine
            gated = gated + mine * gates[:, e : e + 1]
        return taken, gated

    taken, gated = slot_at(lane)
    taken = jnp.where(lane < SLOTS, taken, 0.0)
    gated = jnp.where(lane < SLOTS, gated, 0.0)
    turned = jnp.concatenate([taken, gated], axis=0).T
    select = turned[:SLOTS, :tokens].astype(BF16)
    right = iota((SLOTS, 2 * tokens), 1) >= tokens
    gate_slot = jnp.sum(jnp.where(right, turned[:SLOTS], 0.0), axis=1, keepdims=True)
    again = lane - tokens
    again = jnp.where(again >= SLOTS, again - SLOTS, again)
    back = jnp.where(
        lane < tokens,
        (place == lane.astype(F32)).astype(F32),
        jnp.where(lane < tokens + 2 * SLOTS, slot_at(again)[0], 0.0),
    ).astype(BF16)
    head_select = dot(select, back[:, :HEAD]).astype(BF16)
    return hit, select, head_select, gate_slot, back


def place_row(routes):
    tokens = routes.shape[1]
    here = jnp.max(jnp.where(routes < EXP_WIN, 1.0, 0.0), axis=0, keepdims=True)
    here = jnp.broadcast_to(here, (8, tokens))
    above = (iota((tokens, tokens), 0) < iota((tokens, tokens), 1)).astype(BF16)
    before = dot(here.astype(BF16), above)
    count = jnp.sum(here, axis=1, keepdims=True)
    order = iota((8, tokens), 1).astype(F32)
    return jnp.where(here > 0.0, before, count + order - before)


def permutation(place, tokens):
    return (iota((tokens, tokens), 0).astype(F32) == place).astype(BF16)


def halves(rows):
    high = rows.astype(BF16)
    low = (rows - high.astype(F32)).astype(BF16)
    return jnp.concatenate([high, low], axis=0)


def kernel(
    sections, n,
    froute_hbm, broute_hbm, flogit_hbm, blogit_hbm, fwd_hbm, bwd_hbm, saved_hbm, gain_hbm,
    wg_hbm, wu_hbm, wd_hbm,
    stack_hbm, back_hbm, balance_hbm,
    froute_ref, broute_ref, flogit_ref, blogit_ref, fwd_ref, bwd_ref, saved_ref, gain_ref,
    wgu, wd, place_out, place_in, head_out, tail_out, head_in,
    halved, back_ref, balance_ref,
    slab, rx, part, pair_in, summed, home, raw, wide, terms, stats,
    w_sem, o_sem, z_send, z_recv, d_send, d_recv, f_send, f_recv,
    p_send, p_recv, h_send, h_recv, s_send, s_recv,
):
    tokens, width = fwd_ref.shape
    hidden = wd.shape[0]
    half = n // 2
    span = half // EXP_WIN
    sec, me = lax.axis_index("section"), lax.axis_index("expert")
    core, mine = lax.rem(me, 2), me // 2
    sibling = me + 1 - 2 * core
    after, ahead = lax.rem(sec + 1, sections), lax.rem(sec + sections - 1, sections)

    joined = wgu.shape[0] == 1
    if joined:
        gate_side, up_side = (wgu.at[0, :, pl.ds(i * hidden, hidden)] for i in range(2))
    else:
        gate_side, up_side = wgu.at[0], wgu.at[1]
    loads = [
        pltpu.make_async_copy(src, dst, w_sem.at[i])
        for i, (src, dst) in enumerate((
            (froute_hbm, froute_ref), (broute_hbm, broute_ref),
            (flogit_hbm, flogit_ref), (blogit_hbm, blogit_ref),
            (fwd_hbm, fwd_ref), (bwd_hbm, bwd_ref), (saved_hbm, saved_ref), (gain_hbm, gain_ref),
            (wg_hbm, gate_side), (wu_hbm, up_side), (wd_hbm, wd),
        ))
    ]
    for load in loads[:8]:
        load.start()

    barrier = pltpu.get_barrier_semaphore()
    for d in range(1, n):
        pl.semaphore_signal(
            barrier, inc=1, device_id={"expert": lax.rem(me + d, n)}, device_id_type=MESH
        )
    for where in (after, ahead):
        pl.semaphore_signal(barrier, inc=1, device_id={"section": where}, device_id_type=MESH)

    loads[0].wait()
    loads[1].wait()
    place_out[0] = place_row(froute_ref[...])
    place_out[1] = place_row(broute_ref[...])
    pl.semaphore_wait(barrier, n + 1)

    def z_copy(which, src, dst, where):
        return pltpu.make_async_remote_copy(
            src_ref=src, dst_ref=dst, send_sem=z_send.at[which], recv_sem=z_recv.at[which],
            device_id={"section": where}, device_id_type=MESH,
        )

    places = [
        z_copy(0, place_out.at[0], place_in.at[0], ahead),
        z_copy(1, place_out.at[1], place_in.at[1], after),
    ]
    heads = [
        z_copy(2, head_out.at[0], head_in.at[0], after),
        z_copy(3, head_out.at[1], head_in.at[1], ahead),
    ]
    tails = [
        z_copy(4, tail_out.at[0], stack_hbm.at[0, pl.ds(HEAD, tokens - HEAD)], after),
        z_copy(5, tail_out.at[1], stack_hbm.at[1, pl.ds(HEAD, tokens - HEAD)], ahead),
    ]
    head_keep = [
        pltpu.make_async_copy(head_in.at[i], stack_hbm.at[i, pl.ds(0, HEAD)], o_sem.at[i])
        for i in range(2)
    ]
    for copy in places:
        copy.start()
    for load in loads[8:]:
        load.start()

    def peer(d):
        return lax.rem(mine + d, half)

    def direct(kind, d):
        other = peer(d)
        return pltpu.make_async_remote_copy(
            src_ref=slab.at[kind, other // span], dst_ref=rx.at[kind, core, mine],
            send_sem=d_send.at[kind, other], recv_sem=d_recv.at[kind, mine],
            device_id={"expert": 2 * other + core}, device_id_type=MESH,
        )

    def arrival(kind, d):
        other = peer(d)
        return pltpu.make_async_remote_copy(
            src_ref=slab.at[kind, 0], dst_ref=rx.at[kind, core, other],
            send_sem=d_send.at[kind, other], recv_sem=d_recv.at[kind, other],
            device_id={"expert": 2 * other + core}, device_id_type=MESH,
        )

    def forward(kind, side, other):
        return pltpu.make_async_remote_copy(
            src_ref=rx.at[kind, side, other], dst_ref=rx.at[kind, side, other],
            send_sem=f_send.at[kind, other], recv_sem=f_recv.at[kind, other],
            device_id={"expert": sibling}, device_id_type=MESH,
        )

    def dispatch(kind):
        for d in range(1, half):
            direct(kind, d).start()
        rx[kind, core, mine] = slab[kind, mine // span]
        forward(kind, core, mine).start()

    def relay(kind):
        for d in range(1, half):
            arrival(kind, d).wait_recv()
            forward(kind, core, peer(d)).start()

    def complete(kind):
        for d in range(half):
            forward(kind, 1 - core, peer(d)).wait_recv()

    def to_slab(kind, rows, at):
        for e in range(EXP_WIN):
            slab[kind, e, :, at] = rows[e * CAP : (e + 1) * CAP].astype(BF16)

    loads[3].wait()
    _, b_select, b_pick, b_gate, b_back = route_tables(broute_ref[...], blogit_ref[...])
    loads[4].wait()
    loads[5].wait()
    sources = (fwd_ref, bwd_ref)
    orders = []
    for which in range(2):
        places[which].wait_recv()
        orders.append(permutation(place_in[which, 0:1], tokens))

    for which in (1, 0):
        def fill_head(at, carry, which=which):
            head_out[which, :, at] = dot(orders[which][:HEAD], sources[which][:, at]).astype(BF16)
            return carry

        columns(width, fill_head, chunk=WIDE)
        heads[which].start()

    loads[6].wait()
    loads[7].wait()

    def gather_saved(at, total):
        rows = dot(b_select, saved_ref[:, at])
        raw[:, at] = rows
        return total + jnp.sum(rows * rows, axis=1, keepdims=True)

    square = columns(width, gather_saved, jnp.zeros((SLOTS, 1), F32), chunk=WIDE)
    saved_inv = lax.rsqrt(square / width + EPSILON)

    def norm_saved(at, carry):
        to_slab(0, raw[:, at] * saved_inv * gain_ref[:, at].astype(F32), at)
        return carry

    columns(width, norm_saved, chunk=WIDE)
    dispatch(0)

    loads[2].wait()
    hit, _, f_pick, f_gate, f_back = route_tables(froute_ref[...], flogit_ref[...])
    back_ref[0] = f_back
    back_ref[1] = b_back
    back_keep = pltpu.make_async_copy(back_ref, back_hbm, o_sem.at[2])
    back_keep.start()

    for which in range(2):
        def fill_tail(at, carry, which=which):
            tail_out[which, :, at] = dot(orders[which][HEAD:], sources[which][:, at]).astype(BF16)
            return carry

        columns(width, fill_tail)

    logits = flogit_ref[...]
    raised = jnp.exp(logits - jnp.max(logits, axis=1, keepdims=True))
    probs = raised / jnp.sum(raised, axis=1, keepdims=True)
    count_row = jnp.sum(hit, axis=0, keepdims=True)
    prob_row = jnp.sum(probs, axis=0, keepdims=True)
    row = iota((8, EXPERTS), 0)
    stats[me] = jnp.where(row == 0, count_row, jnp.where(row == 1, prob_row, 0.0))

    def stat(d):
        other = lax.rem(me + d, n)
        return pltpu.make_async_remote_copy(
            src_ref=stats.at[me], dst_ref=stats.at[me],
            send_sem=s_send.at[other], recv_sem=s_recv.at[me],
            device_id={"expert": other}, device_id_type=MESH,
        )

    def stat_arrival(d):
        other = lax.rem(me + d, n)
        return pltpu.make_async_remote_copy(
            src_ref=stats.at[other], dst_ref=stats.at[other],
            send_sem=s_send.at[other], recv_sem=s_recv.at[other],
            device_id={"expert": other}, device_id_type=MESH,
        )

    for d in range(1, n):
        stat(d).start()

    def arrived(kind, at):
        return rx[kind, :, :, :, at].astype(F32).reshape(n * CAP, CHUNK).astype(BF16)

    zero = jnp.zeros((n * CAP, hidden), F32)

    def gate_up(kind):
        def step(at, totals):
            rows = arrived(kind, at)
            return tuple(total + dot(rows, wgu[i, at, :]) for i, total in enumerate(totals))

        empty = jnp.zeros((n * CAP, wgu.shape[2]), F32)
        totals = columns(width, step, (empty,) * wgu.shape[0])
        return (totals[0][:, :hidden], totals[0][:, hidden:]) if joined else totals

    relay(0)

    heads[1].wait_recv()
    heads[0].wait_recv()
    for copy in tails:
        copy.start()
    for copy in head_keep:
        copy.start()


    def gather_grads(at, carry):
        to_slab(1, dot(b_pick, head_in[1, :, at]) * b_gate, at)
        return carry

    columns(width, gather_grads, chunk=WIDE)
    dispatch(1)


    def gather_fwd(at, total):
        rows = dot(f_pick, head_in[0, :, at])
        wide[:, at] = rows
        return total + jnp.sum(rows * rows, axis=1, keepdims=True)

    square = columns(width, gather_fwd, jnp.zeros((SLOTS, 1), F32), chunk=WIDE)
    fwd_inv = lax.rsqrt(square / width + EPSILON)

    def norm_fwd(at, carry):
        to_slab(2, wide[:, at] * fwd_inv * gain_ref[:, at].astype(F32), at)
        return carry

    columns(width, norm_fwd, chunk=WIDE)
    dispatch(2)

    loads[8].wait()
    loads[9].wait()
    complete(0)
    gate_b, up_b = gate_up(0)
    sigma = jax.nn.sigmoid(gate_b)
    terms[0] = up_b * sigma * (1.0 + gate_b * (1.0 - sigma))
    terms[1] = gate_b * sigma
    relay(1)
    loads[10].wait()
    complete(1)

    piece = width // PIECES

    def pair(which, p):
        return pltpu.make_async_remote_copy(
            src_ref=part.at[which, p, 1 - core], dst_ref=pair_in.at[which, p],
            send_sem=p_send.at[which, p], recv_sem=p_recv.at[which, p],
            device_id={"expert": sibling}, device_id_type=MESH,
        )

    def to_home(which, p, d):
        other = peer(d)
        return pltpu.make_async_remote_copy(
            src_ref=summed.at[which, p, other], dst_ref=home.at[which, p, mine],
            send_sem=h_send.at[which, p, other], recv_sem=h_recv.at[which, p, mine],
            device_id={"expert": 2 * other + core}, device_id_type=MESH,
        )

    def from_holder(which, p, d):
        other = peer(d)
        return pltpu.make_async_remote_copy(
            src_ref=summed.at[which, p, other], dst_ref=home.at[which, p, other],
            send_sem=h_send.at[which, p, other], recv_sem=h_recv.at[which, p, other],
            device_id={"expert": 2 * other + core}, device_id_type=MESH,
        )

    def make_piece(which, p, make):
        rows = make(pl.ds(p * piece, piece))
        part[which, p] = rows.reshape(2, half, CAP, piece).astype(BF16)
        pair(which, p).start()

    def give(which, p):
        pair(which, p).wait_recv()

        def add(at, carry):
            total = part[which, p, core, :, :, at].astype(F32)
            total = total + pair_in[which, p, :, :, at].astype(F32)
            summed[which, p, :, :, at] = total.astype(BF16)
            return carry

        columns(piece, add)
        for d in range(1, half):
            to_home(which, p, d).start()
        home[which, p, mine] = summed[which, p, mine]

    d_hidden = columns(
        width,
        lambda at, total: total
        + lax.dot_general(arrived(1, at), wd[:, at], NT, preferred_element_type=F32),
        zero,
    )
    d_parts = [(d_hidden * terms[i]).astype(BF16) for i in range(2)]
    if joined:
        d_parts = [jnp.concatenate(d_parts, axis=1)]

    def input_grad(at):
        return sum(
            lax.dot_general(d_part, wgu[i, at, :], NT, preferred_element_type=F32)
            for i, d_part in enumerate(d_parts)
        )

    relay(2)
    make_piece(0, 0, input_grad)
    make_piece(0, 1, input_grad)
    give(0, 0)
    for p in range(2, PIECES):
        make_piece(0, p, input_grad)
        give(0, p - 1)
    complete(2)
    gate_f, up_f = gate_up(2)
    hidden_rows = (gate_f * jax.nn.sigmoid(gate_f) * up_f).astype(BF16)
    give(0, PIECES - 1)

    def down(at):
        return dot(hidden_rows, wd[:, at])

    make_piece(1, 0, down)
    for p in range(1, PIECES):
        make_piece(1, p, down)
        give(1, p - 1)
    give(1, PIECES - 1)

    for d in range(1, n):
        stat_arrival(d).wait_recv()
    counts = stats[0]
    for i in range(1, n):
        counts = counts + stats[i]
    tokens_all = tokens * n
    balance_ref[...] = (
        EXPERTS * (counts[0:1] / (tokens_all * TOPK)) * (counts[1:2] / tokens_all)
    )
    balance_keep = pltpu.make_async_copy(balance_ref, balance_hbm, o_sem.at[3])
    balance_keep.start()

    def returned(which, p, at):
        rows = []
        for e in range(EXP_WIN):
            total = home[which, p, e * span, :, at].astype(F32)
            for i in range(1, span):
                total = total + home[which, p, e * span + i, :, at].astype(F32)
            rows.append(total)
        return jnp.concatenate(rows, axis=0)

    def by_piece(which, p, step, init):
        for d in range(1, half):
            from_holder(which, p, d).wait_recv()

        at = pl.ds(0, piece)
        return step(pl.ds(p * piece, piece), returned(which, p, at), init)

    def weigh(at, rows, total):
        weighted = rows * gain_ref[:, at].astype(F32)
        wide[:, at] = weighted
        return total + jnp.sum(weighted * raw[:, at], axis=1, keepdims=True)

    total = jnp.zeros((SLOTS, 1), F32)
    for p in range(PIECES):
        total = by_piece(0, p, weigh, total)
    scale = saved_inv * saved_inv * saved_inv * (total / width)

    def rows_copy(which, at, i):
        rows = pl.ds(tokens, 2 * SLOTS)
        return pltpu.make_async_copy(
            halved.at[which, :, at], stack_hbm.at[which, rows, at], o_sem.at[4 + i]
        )

    def finish_bwd(at, carry):
        rows = saved_inv * wide[:, at] - raw[:, at] * scale
        halved[1, :, at] = halves(rows)
        return carry

    columns(width, finish_bwd, chunk=WIDE)
    kept = [rows_copy(1, pl.ds(0, width), PIECES)]
    kept[0].start()

    def finish_fwd(at, rows, carry):
        halved[0, :, at] = halves(rows * f_gate)
        return carry

    for p in range(PIECES):
        by_piece(1, p, finish_fwd, 0)
        kept.append(rows_copy(0, pl.ds(p * piece, piece), p))
        kept[-1].start()

    for copy in tails:
        copy.wait_recv()
    for copy in head_keep + [back_keep, balance_keep] + kept:
        copy.wait()
    for copy in places + heads + tails:
        copy.wait_send()
    for kind in range(3):
        for d in range(half):
            forward(kind, core, peer(d)).wait_send()
        for d in range(1, half):
            direct(kind, d).wait_send()
    for which in range(2):
        for p in range(PIECES):
            pair(which, p).wait_send()
            for d in range(1, half):
                to_home(which, p, d).wait_send()
    for d in range(1, n):
        stat(d).wait_send()


def place_kernel(
    stack_hbm, back_hbm, balance_hbm, fout_hbm, bout_hbm, out_hbm,
    stack, back, balance, out, in_sem, out_sem, small_sem,
):
    _, rows, width = stack.shape
    steps = width // CHUNK
    spans = [pl.ds(i * CHUNK, CHUNK) for i in range(steps)]
    small = [
        pltpu.make_async_copy(back_hbm, back, small_sem.at[0]),
        pltpu.make_async_copy(balance_hbm, balance, small_sem.at[1]),
    ]
    loads = [
        pltpu.make_async_copy(stack_hbm.at[:, :, at], stack.at[:, :, at], in_sem.at[i])
        for i, at in enumerate(spans)
    ]
    for copy in small + loads:
        copy.start()
    small[1].wait()
    last = pltpu.make_async_copy(balance, out_hbm, small_sem.at[2])
    last.start()
    small[0].wait()
    stores = []
    for i, at in enumerate(spans):
        loads[i].wait()
        for which, target in enumerate((fout_hbm, bout_hbm)):
            out[which, :, at] = dot(back[which, :, :rows], stack[which, :, at]).astype(BF16)
            store = pltpu.make_async_copy(
                out.at[which, :, at], target.at[:, at], out_sem.at[which, i]
            )
            store.start()
            stores.append(store)
    for copy in stores + [last]:
        copy.wait()


def body(
    sections, n,
    fwd_sent, bwd_sent, bwd_saved, fwd_routes, bwd_routes, fwd_logits, bwd_logits,
    norm_gain, w_gate, w_up, w_down,
):
    tokens, width = fwd_sent.shape[1:]
    hidden = w_gate.shape[2]
    half = n // 2
    hbm = pl.BlockSpec(memory_space=pl.ANY)
    dma = pltpu.SemaphoreType.DMA
    rows = tokens + 2 * SLOTS
    stack, back, balance = pl.pallas_call(
        functools.partial(kernel, sections, n),
        out_shape=(
            jax.ShapeDtypeStruct((2, rows, width), BF16),
            jax.ShapeDtypeStruct((2, tokens, EXPERTS), BF16),
            jax.ShapeDtypeStruct((1, EXPERTS), F32),
        ),
        in_specs=[hbm] * 11,
        out_specs=(hbm, hbm, hbm),
        scratch_shapes=[
            pltpu.VMEM((TOPK, tokens), jnp.int32),
            pltpu.VMEM((TOPK, tokens), jnp.int32),
            pltpu.VMEM((tokens, EXPERTS), F32),
            pltpu.VMEM((tokens, EXPERTS), F32),
            pltpu.VMEM((tokens, width), BF16),
            pltpu.VMEM((tokens, width), BF16),
            pltpu.VMEM((tokens, width), BF16),
            pltpu.VMEM((1, width), BF16),
            pltpu.VMEM((1, width, 2 * hidden) if hidden % 128 == 0 else (2, width, hidden), BF16),
            pltpu.VMEM((hidden, width), BF16),
            pltpu.VMEM((2, 8, tokens), F32),
            pltpu.VMEM((2, 8, tokens), F32),
            pltpu.VMEM((2, HEAD, width), BF16),
            pltpu.VMEM((2, tokens - HEAD, width), BF16),
            pltpu.VMEM((2, HEAD, width), BF16),
            pltpu.VMEM((2, 2 * SLOTS, width), BF16),
            pltpu.VMEM((2, tokens, EXPERTS), BF16),
            pltpu.VMEM((1, EXPERTS), F32),
            pltpu.VMEM((3, EXP_WIN, CAP, width), BF16),
            pltpu.VMEM((3, 2, half, CAP, width), BF16),
            pltpu.VMEM((2, PIECES, 2, half, CAP, width // PIECES), BF16),
            pltpu.VMEM((2, PIECES, half, CAP, width // PIECES), BF16),
            pltpu.VMEM((2, PIECES, half, CAP, width // PIECES), BF16),
            pltpu.VMEM((2, PIECES, half, CAP, width // PIECES), BF16),
            pltpu.VMEM((SLOTS, width), F32),
            pltpu.VMEM((SLOTS, width), F32),
            pltpu.VMEM((2, n * CAP, hidden), F32),
            pltpu.VMEM((n, 8, EXPERTS), F32),
            dma((11,)), dma((5 + PIECES,)), dma((6,)), dma((6,)),
            dma((3, half)), dma((3, half)), dma((3, half)), dma((3, half)),
            dma((2, PIECES)), dma((2, PIECES)), dma((2, PIECES, half)), dma((2, PIECES, half)),
            dma((n,)), dma((n,)),
        ],
        compiler_params=pltpu.CompilerParams(
            collective_id=0, has_side_effects=True, vmem_limit_bytes=60 * 1024 * 1024
        ),
    )(
        fwd_routes[0].T, bwd_routes[0].T, fwd_logits[0], bwd_logits[0],
        fwd_sent[0], bwd_sent[0], bwd_saved[0], norm_gain, w_gate[0], w_up[0], w_down[0],
    )
    fwd_out, bwd_out, balance = pl.pallas_call(
        place_kernel,
        out_shape=(
            jax.ShapeDtypeStruct((tokens, width), BF16),
            jax.ShapeDtypeStruct((tokens, width), BF16),
            jax.ShapeDtypeStruct((1, EXPERTS), F32),
        ),
        in_specs=[hbm] * 3,
        out_specs=(hbm, hbm, hbm),
        scratch_shapes=[
            pltpu.VMEM((2, rows, width), BF16),
            pltpu.VMEM((2, tokens, EXPERTS), BF16),
            pltpu.VMEM((1, EXPERTS), F32),
            pltpu.VMEM((2, tokens, width), BF16),
            dma((width // CHUNK,)), dma((2, width // CHUNK)), dma((3,)),
        ],
        compiler_params=pltpu.CompilerParams(vmem_limit_bytes=60 * 1024 * 1024),
    )(stack, back, balance)
    return fwd_out[None], bwd_out[None], balance


def solution(mesh):
    block = P("section", "expert", None)
    return jax.shard_map(
        functools.partial(body, mesh.shape["section"], mesh.shape["expert"]),
        mesh=mesh,
        in_specs=(block,) * 7
        + (
            P("section", None),
            P("section", None, "expert"),
            P("section", None, "expert"),
            P("section", "expert", None),
        ),
        out_specs=(block, block, P("section", None)),
        check_vma=False,
    )
```
